128 devices in a mesh: seq: 32 (over y, z, core), tp: 4 (over x).
Axes of the slice: x: 4, y: 4, z: 4, core: 2. Of those that a mesh axis runs over, the one named last changes fastest.
Arguments:
- tokens: bfloat16 [16384, 4096], P('seq', 'tp'), may hold values from -18 to 18
- weights: bfloat16 [3, 4096, 4096], P(None, 'seq', 'tp'), may hold values from -0.09375 to 0.09375
- gate_bias: float32 [3, 4096], P(None, 'tp'), may hold values from -16 to 8
- recurrent: float32 [3, 4096], P(None, 'tp'), may hold values from -0.5 to 0.5
- initial_state: float32 [4096], P('tp'), may hold values from -3 to 3
Outputs:
- states: float32 [16384, 4096], P('seq', 'tp')
The draws below stay inside these ranges and needn't reach their ends.
All inputs are finite; a program needn't handle non-finite values.
Results may differ from the reference program's by a relative error of at most 0.0003.
Values may be sent and summed in bfloat16 or wider, within the bound.
A program may use at most 128 MiB of HBM per device.

```python
import jax
import jax.numpy as jnp
from jax import lax

D = 4096
ITERS = 2
WINDOW_TOKENS = 16384


def draw_tokens(key, part):
    key = jax.random.fold_in(key, 11)
    root_random_key, spike_random_key = jax.random.split(key, 2)
    values = jax.random.normal(root_random_key, (WINDOW_TOKENS, D), jnp.float32)
    spike_token_rows = jax.random.randint(spike_random_key, (8,), 0, WINDOW_TOKENS)
    flagged_positions = jnp.any(jnp.arange(WINDOW_TOKENS)[:, None] == spike_token_rows[None, :], axis=1)
    values = values * jnp.where(flagged_positions, 6.0, 1.0)[:, None]
    return jnp.clip(values, -18.0, 18.0).astype(jnp.bfloat16)


def draw_gate_bias(key, part):
    key = jax.random.fold_in(key, 23)
    pick_key, gradual_random_key, fast_key, other_key = jax.random.split(key, 4)
    share = 0.5
    slow_rate = jnp.exp(jax.random.uniform(gradual_random_key, (D,), jnp.float32, jnp.log(0.1 / WINDOW_TOKENS), jnp.log(1.0 / WINDOW_TOKENS)))
    fast_rate = jnp.exp(jax.random.uniform(fast_key, (D,), jnp.float32, jnp.log(1.0 / 50.0), jnp.log(1.0 / 10.0)))
    chosen = jax.random.uniform(pick_key, (D,), jnp.float32) < share
    rate = jnp.where(chosen, slow_rate, fast_rate)
    update_bias = jnp.log(rate) - jnp.log1p(-rate)
    others = jax.random.normal(other_key, (2, D), jnp.float32) * jnp.array([[1.0], [0.5]]) + jnp.array([[1.0], [0.3]])
    others = jnp.clip(others, -4.0, 6.0)
    return jnp.concatenate([update_bias[None, :], others], axis=0).astype(jnp.float32)


def block_levels(stream_key, shape, shards, smallest, high):
    def one(position, shards_of):
        steps = jax.random.uniform(jax.random.fold_in(jax.random.fold_in(stream_key, 6), position), (shards_of,), jnp.float32, smallest / len(shards), high / len(shards))
        return jnp.repeat(jnp.exp(steps), shape[position] // shards_of).reshape((-1,) + (1,) * (len(shape) - position - 1))

    factor_of = one(*shards[0])
    for cut in shards[1:]:
        factor_of = factor_of * one(*cut)
    return factor_of


def centred(own_key, dims, spread, bound, pieces=(), dtype=jnp.bfloat16):
    loudness = block_levels(own_key, dims, pieces, -0.22, 0.18) if pieces else 1.0
    values = jax.random.normal(own_key, dims, jnp.float32) * spread * loudness
    return jnp.minimum(jnp.maximum(values, -bound), bound).astype(dtype)


def setup_inputs(seed: int = 0) -> dict:
    key_of = jax.random.split(jax.random.key(seed), 6)
    return {
        "tokens": draw_tokens(jax.random.fold_in(key_of[5], 71), 0),
        "weights": centred(key_of[1], (3, D, D), D ** -0.5, 0.09375, ((1, 32), (2, 4))),
        "gate_bias": draw_gate_bias(jax.random.fold_in(key_of[5], 71), 0),
        "recurrent": jnp.clip(jax.random.uniform(key_of[3], (3, D), jnp.float32, -0.5, 0.5) * block_levels(key_of[3], (3, D), ((1, 4),), -0.4, 0.0), -0.5, 0.5),
        "initial_state": centred(key_of[4], (D,), 0.7, 3.0, ((0, 4),), jnp.float32),
    }


def cell_terms(preact, previous, coeffs):
    update_gate = jax.nn.sigmoid(preact[0] + coeffs[0] * previous)
    reset_gate = jax.nn.sigmoid(preact[1] + coeffs[1] * previous)
    candidate = jnp.tanh(preact[2] + coeffs[2] * reset_gate * previous)
    stepped = (1.0 - update_gate) * previous + update_gate * candidate
    update_slope = update_gate * (1.0 - update_gate) * coeffs[0]
    reset_slope = reset_gate * (1.0 - reset_gate) * coeffs[1]
    candidate_slope = (1.0 - candidate * candidate) * coeffs[2] * (reset_gate + previous * reset_slope)
    jacobian = (1.0 - update_gate) + (candidate - previous) * update_slope + update_gate * candidate_slope
    return stepped, jacobian


def compose(earlier, later):
    return (earlier[0] * later[0], later[0] * earlier[1] + later[1])


def reference(tokens, weights, gate_bias, recurrent, initial_state):
    block_width = min(512, D)
    block_count = D // block_width
    weight_blocks = weights.reshape(3, D, block_count, block_width).transpose(2, 0, 1, 3)
    bias_blocks = gate_bias.reshape(3, block_count, block_width).transpose(1, 0, 2)
    coeff_blocks = recurrent.reshape(3, block_count, block_width).transpose(1, 0, 2)
    init_blocks = initial_state.reshape(block_count, block_width)

    def solve_block(packed):
        weight_block, bias_block, coeff_block, init_block = packed
        preact = jnp.stack([jnp.dot(tokens, weight_block[g], preferred_element_type=jnp.float32) for g in range(3)])
        preact = preact + bias_block[:, None, :]
        state = jnp.zeros((WINDOW_TOKENS, block_width), jnp.float32)
        for iteration in range(ITERS):
            previous = jnp.concatenate([init_block[None, :], state[:-1]], axis=0)
            stepped, jacobian = cell_terms(preact, previous, coeff_block[:, None, :])
            offset = stepped - jacobian * previous
            offset = offset.at[0].add(jacobian[0] * init_block)
            state = lax.associative_scan(compose, (jacobian, offset), axis=0)[1]
        return state

    solved = lax.map(solve_block, (weight_blocks, bias_blocks, coeff_blocks, init_blocks))
    return solved.transpose(1, 0, 2).reshape(WINDOW_TOKENS, D)
```

```python
import functools

import jax
import jax.numpy as jnp
from jax import lax
from jax.experimental import pallas as pl
from jax.experimental.pallas import tpu as pltpu
from jax.sharding import PartitionSpec as P

MESH = pl.DeviceIdType.MESH
RING = 4
CHIPS = RING * RING
CH = 128
CHUNKS = 4
TOK = 512
ROWS = 2 * TOK
FEAT = 1024
DEPTH = CHIPS * 256
SEGS = 8
SEG = ROWS // SEGS


def sigmoid(v):
    return jax.nn.sigmoid(v)


def cell(pre, p, coef):
    u = sigmoid(pre[0] + coef[0] * p)
    r = sigmoid(pre[1] + coef[1] * p)
    c = jnp.tanh(pre[2] + coef[2] * r * p)
    keep = 1.0 - u
    slope = c - p
    jac = (
        keep
        + slope * (u * keep * coef[0])
        + u * ((1.0 - c * c) * coef[2]) * (r + p * (r * (1.0 - r) * coef[1]))
    )
    stepped = keep * p + u * c
    return jac, stepped - jac * p


def cell_at_zero(pre, coef):
    u = sigmoid(pre[0])
    r = sigmoid(pre[1])
    c = jnp.tanh(pre[2])
    keep = 1.0 - u
    jac = keep + c * (u * keep * coef[0]) + u * ((1.0 - c * c) * coef[2]) * r
    return jac, u * c


def kernel(
    tok_hbm, w_hbm, bias, rec, init, out_hbm,
    X, W, PRE, AB1, AB2, OUTB, SEGT, SUM, SLOT,
    local_sem, sib_s, sib_r, p1_s, p1_r, p2_s, p2_r, t_s, t_r, ts_s, ts_r,
    ex_s, ex_r, o_l, o_s, o_r,
):
    seq, x = lax.axis_index("seq"), lax.axis_index("tp")
    c = lax.rem(seq, 2)
    q = seq // 2
    y, z = q // RING, lax.rem(q, RING)
    p = (1 - c) * y + c * z
    s = (1 - c) * z + c * y

    def block(pp, ss):
        return lax.rem(pp, RING) * (4 - 3 * c) + lax.rem(ss, RING) * (1 + 3 * c)

    def peer(qq):
        return (qq * 2 + c, x)

    right, left = peer(block(p + 1, s)), peer(block(p + 3, s))
    up, down = peer(block(p, s + 1)), peer(block(p, s + 3))
    xr, xl = (seq, lax.rem(x + 1, RING)), (seq, lax.rem(x + 3, RING))
    sib = (q * 2 + 1 - c, x)

    barrier = pltpu.get_barrier_semaphore()

    def greet(e, _):
        pl.semaphore_signal(
            barrier, inc=1, device_id=peer(lax.rem(q + e, CHIPS)), device_id_type=MESH
        )
        return 0

    lax.fori_loop(1, CHIPS, greet, 0)
    for d in (xr, xl, sib):
        pl.semaphore_signal(barrier, inc=1, device_id=d, device_id_type=MESH)
    pl.semaphore_wait(barrier, CHIPS + 2)

    def rcopy(src, dst, ss, rs, dev):
        return pltpu.make_async_remote_copy(
            src_ref=src, dst_ref=dst, send_sem=ss, recv_sem=rs, device_id=dev, device_id_type=MESH
        )

    sends = []

    def send(ref, ss, rs, dev, dst=None):
        cp = rcopy(ref, ref if dst is None else dst, ss, rs, dev)
        cp.start()
        sends.append((ref if dst is None else dst, ss))

    def arrived(ref, sem):
        pltpu.make_async_copy(ref, ref, sem).wait()

    def wrows(k, blk, half=None):
        start = blk * 256
        if half is None:
            return W.at[k, pl.ds(pl.multiple_of(start, 256), 256)]
        return W.at[k, pl.ds(pl.multiple_of(start + half * 128, 128), 128)]

    def chan(core, k):
        return pl.ds(pl.multiple_of(core * (CH * CHUNKS) + k * CH, CH), CH)

    for k in range(CHUNKS):
        for g in range(3):
            lanes = pl.ds(g * CH, CH)
            mine = pl.ds(pl.multiple_of(q * 256 + c * 128, 128), 128)
            pltpu.make_async_copy(
                w_hbm.at[g, :, chan(c, k)], W.at[k, mine, lanes], local_sem.at[k]
            ).start()
            rcopy(
                w_hbm.at[g, :, chan(1 - c, k)], W.at[k, mine, lanes], sib_s.at[k], sib_r.at[k], sib
            ).start()

    def trows(core, half=None):
        if half is None:
            return pl.ds(pl.multiple_of(core * TOK, TOK), TOK)
        return pl.ds(pl.multiple_of(core * TOK + half * 256, 256), 256)

    def tcols(xx):
        return pl.ds(pl.multiple_of(lax.rem(xx, RING) * FEAT, FEAT), FEAT)

    own_tok = pltpu.make_async_copy(tok_hbm, X.at[trows(c), tcols(x)], local_sem.at[CHUNKS])
    own_tok.start()

    for k in range(CHUNKS):
        own_half = wrows(k, q, c)
        arrived(own_half, local_sem.at[k])
        arrived(wrows(k, q, 1 - c), sib_r.at[k])
        piece = wrows(k, q)
        send(piece, p1_s.at[k, 0], p1_r.at[k, 0], right)
        send(piece, p1_s.at[k, 1], p1_r.at[k, 1], left)
    own_tok.wait()
    own_piece = X.at[trows(c), tcols(x)]
    send(own_piece, t_s.at[0], t_r.at[0], xr)
    send(own_piece, t_s.at[1], t_r.at[1], xl)
    send(own_piece, ts_s.at[0], ts_r.at[0], sib)

    def send2(k, i):
        piece = wrows(k, block(p + i, s))
        send(piece, p2_s.at[k, i, 0], p2_r.at[k, i, 0], up)
        send(piece, p2_s.at[k, i, 1], p2_r.at[k, i, 1], down)

    send2(0, 0)
    for k in range(CHUNKS):
        arrived(wrows(k, block(p + 3, s)), p1_r.at[k, 0])
        send(wrows(k, block(p + 3, s), 0), p1_s.at[k, 2], p1_r.at[k, 2], right)
        arrived(wrows(k, block(p + 1, s)), p1_r.at[k, 1])
        send(wrows(k, block(p + 1, s), 1), p1_s.at[k, 3], p1_r.at[k, 3], left)
        if k == 0:
            send2(0, 3)
            send2(0, 1)

    def row_of(ref, g, k):
        return ref[pl.ds(g, 1), chan(c, k)]

    def matmul(k):
        par = k % 2

        def tile(m, _):
            rows = pl.ds(pl.multiple_of(m * 256, 256), 256)
            acc = jnp.dot(X[rows, :], W[k], preferred_element_type=jnp.float32)
            for g in range(3):
                v = acc[:, g * CH : (g + 1) * CH] + row_of(bias, g, k)
                for h in range(2):
                    PRE[par, g, pl.ds(m * 2 + h, SEG, stride=SEGS), :] = v[h * SEG : (h + 1) * SEG]
            return 0

        lax.fori_loop(0, ROWS // 256, tile, 0)

    def vreg(j):
        return pl.ds(pl.multiple_of(j * SEGS, SEGS), SEGS)

    sublane = lax.broadcasted_iota(jnp.int32, (SEGS, CH), 0)

    def coefs(k):
        return [jnp.broadcast_to(row_of(rec, g, k), (SEGS, CH)) for g in range(3)]

    def publish(n, A, B):
        SEGT[n, 0] = A
        SEGT[n, 1] = B
        ta, tb = SEGT[n, 0, 0:1], SEGT[n, 1, 0:1]
        for i in range(1, SEGS):
            a, b = SEGT[n, 0, i : i + 1], SEGT[n, 1, i : i + 1]
            ta, tb = a * ta, a * tb + b
        SUM[n] = jnp.where(sublane == 0, ta, tb)

        def one(e, _):
            rcopy(
                SUM.at[n], SLOT.at[n, e], ex_s.at[n], ex_r.at[n], peer(lax.rem(q + e, CHIPS))
            ).start()
            return 0

        lax.fori_loop(1, CHIPS, one, 0)

    def incoming(n, k):
        arrived(SLOT.at[n, pl.ds(1, CHIPS - 1)], ex_r.at[n])

        def one(i, h):
            return SLOT[n, q - i, 0:1] * h + SLOT[n, q - i, 1:2]

        h = lax.fori_loop(0, q, one, row_of(init, 0, k))
        SEGT[n, 2, 0:1] = h
        for i in range(SEGS - 1):
            h = SEGT[n, 0, i : i + 1] * h + SEGT[n, 1, i : i + 1]
            SEGT[n, 2, i + 1 : i + 2] = h
        return SEGT[n, 2]

    UN = 8

    def pass1(k):
        par = k % 2
        coef = coefs(k)
        first = (sublane + q) == 0
        p0 = jnp.where(first, jnp.broadcast_to(row_of(init, 0, k), (SEGS, CH)), 0.0)
        A, B = cell([PRE[par, g, vreg(0), :] for g in range(3)], p0, coef)
        AB1[0, vreg(0), :] = A
        AB1[1, vreg(0), :] = B

        def step(j, A, B):
            a, b = cell_at_zero([PRE[par, g, vreg(j), :] for g in range(3)], coef)
            AB1[0, vreg(j), :] = a
            AB1[1, vreg(j), :] = b
            return a * A, a * B + b

        for j in range(1, UN):
            A, B = step(j, A, B)

        def group(t, AB):
            A, B = AB
            for o in range(UN):
                A, B = step(t * UN + o, A, B)
            return A, B

        A, B = lax.fori_loop(1, SEG // UN, group, (A, B))
        publish(2 * k, A, B)

    def pass2(k):
        par = k % 2
        coef = coefs(k)
        h = incoming(2 * k, k)

        def group(t, carry):
            h, A, B = carry
            for o in range(UN):
                v = vreg(t * UN + o)
                a, b = cell([PRE[par, g, v, :] for g in range(3)], h, coef)
                AB2[0, v, :] = a
                AB2[1, v, :] = b
                h = AB1[0, v, :] * h + AB1[1, v, :]
                A, B = a * A, a * B + b
            return h, A, B

        one, zero = jnp.ones((SEGS, CH), jnp.float32), jnp.zeros((SEGS, CH), jnp.float32)
        _, A, B = lax.fori_loop(0, SEG // UN, group, (h, one, zero))
        publish(2 * k + 1, A, B)

    def pass3(k):
        h = incoming(2 * k + 1, k)

        def group(t, h):
            for o in range(UN):
                j = t * UN + o
                v = vreg(j)
                h = AB2[0, v, :] * h + AB2[1, v, :]
                OUTB[k, pl.ds(j, SEGS, stride=SEG), :] = h
            return h

        lax.fori_loop(0, SEG // UN, group, h)
        here = out_hbm.at[:, chan(c, k)]
        pltpu.make_async_copy(OUTB.at[k, trows(c)], here, o_l.at[k]).start()
        rcopy(OUTB.at[k, trows(1 - c)], here, o_s.at[k], o_r.at[k], sib).start()

    def features_on():
        arrived(X.at[trows(c), tcols(x + 3)], t_r.at[0])
        send(X.at[trows(c, 0), tcols(x + 3)], t_s.at[2], t_r.at[2], xr)
        arrived(X.at[trows(c), tcols(x + 1)], t_r.at[1])
        send(X.at[trows(c, 1), tcols(x + 1)], t_s.at[3], t_r.at[3], xl)
        send(X.at[trows(c), tcols(x + 3)], ts_s.at[1], ts_r.at[1], sib)
        send(X.at[trows(c), tcols(x + 1)], ts_s.at[2], ts_r.at[2], sib)

    def features_end():
        for h in range(2):
            arrived(X.at[trows(c, h), tcols(x + 2)], t_r.at[2 + h])
            send(X.at[trows(c, h), tcols(x + 2)], ts_s.at[3 + h], ts_r.at[3 + h], sib)
        arrived(X.at[trows(1 - c), tcols(x)], ts_r.at[0])
        arrived(X.at[trows(1 - c), tcols(x + 3)], ts_r.at[1])
        arrived(X.at[trows(1 - c), tcols(x + 1)], ts_r.at[2])
        for h in range(2):
            arrived(X.at[trows(1 - c, h), tcols(x + 2)], ts_r.at[3 + h])

    def last_of_group(k):
        for h in range(2):
            arrived(wrows(k, block(p + 2, s), h), p1_r.at[k, 2 + h])
        if k > 0:
            for i in (0, 3, 1):
                send2(k, i)
        send2(k, 2)

    def pass_on(k):
        for i in (0, 3, 1, 2):
            arrived(wrows(k, block(p + i, s + 3)), p2_r.at[k, i, 0])
            send(wrows(k, block(p + i, s + 3), 0), p2_s.at[k, i, 2], p2_r.at[k, i, 2], up)
            arrived(wrows(k, block(p + i, s + 1)), p2_r.at[k, i, 1])
            send(wrows(k, block(p + i, s + 1), 1), p2_s.at[k, i, 3], p2_r.at[k, i, 3], down)

    def gathered(k):
        for i in range(RING):
            for h in range(2):
                arrived(wrows(k, block(p + i, s + 2), h), p2_r.at[k, i, 2 + h])

    last_of_group(0)
    for k in range(CHUNKS + 1):
        if k + 1 < CHUNKS:
            last_of_group(k + 1)
        if k < CHUNKS:
            pass_on(k)
        if k == 0:
            features_on()
        if k == 1:
            features_end()
        if k >= 1:
            gathered(k - 1)
            matmul(k - 1)
            pass1(k - 1)
            if k >= 2:
                pass3(k - 2)
            pass2(k - 1)
    pass3(CHUNKS - 1)

    for k in range(CHUNKS):
        here = out_hbm.at[:, chan(c, k)]
        there = out_hbm.at[:, chan(1 - c, k)]
        arrived(here, o_l.at[k])
        arrived(here, o_s.at[k])
        arrived(there, o_r.at[k])
        arrived(wrows(k, q, 0), sib_s.at[k])
    for ref, sem in sends:
        arrived(ref, sem)
    for n in range(2 * CHUNKS):
        arrived(SLOT.at[n, pl.ds(1, CHIPS - 1)], ex_s.at[n])


def body(tokens, weights, gate_bias, recurrent, initial_state):
    dma = pltpu.SemaphoreType.DMA
    f32, bf16 = jnp.float32, jnp.bfloat16
    vmem, hbm = pl.BlockSpec(memory_space=pltpu.VMEM), pl.BlockSpec(memory_space=pl.ANY)
    return pl.pallas_call(
        kernel,
        out_shape=jax.ShapeDtypeStruct((TOK, 2 * CH * CHUNKS), f32),
        in_specs=[hbm, hbm, vmem, vmem, vmem],
        out_specs=hbm,
        scratch_shapes=[
            pltpu.VMEM((ROWS, DEPTH), bf16),
            pltpu.VMEM((CHUNKS, DEPTH, 3 * CH), bf16),
            pltpu.VMEM((2, 3, ROWS, CH), f32),
            pltpu.VMEM((2, ROWS, CH), f32),
            pltpu.VMEM((2, ROWS, CH), f32),
            pltpu.VMEM((CHUNKS, ROWS, CH), f32),
            pltpu.VMEM((2 * CHUNKS, 3, SEGS, CH), f32),
            pltpu.VMEM((2 * CHUNKS, SEGS, CH), f32),
            pltpu.VMEM((2 * CHUNKS, CHIPS, SEGS, CH), f32),
            dma((CHUNKS + 1,)),
            dma((CHUNKS,)),
            dma((CHUNKS,)),
            dma((CHUNKS, 4)),
            dma((CHUNKS, 4)),
            dma((CHUNKS, RING, 4)),
            dma((CHUNKS, RING, 4)),
            dma((4,)),
            dma((4,)),
            dma((5,)),
            dma((5,)),
            dma((2 * CHUNKS,)),
            dma((2 * CHUNKS,)),
            dma((CHUNKS,)),
            dma((CHUNKS,)),
            dma((CHUNKS,)),
        ],
        compiler_params=pltpu.CompilerParams(
            collective_id=0, has_side_effects=True, vmem_limit_bytes=56 * 2**20
        ),
        cost_estimate=pl.CostEstimate(
            flops=2 * ROWS * DEPTH * 3 * CH * CHUNKS, bytes_accessed=8 * 2**20, transcendentals=0
        ),
    )(tokens, weights, gate_bias, recurrent, initial_state[None, :])


def solution(mesh):
    return jax.shard_map(
        body,
        mesh=mesh,
        in_specs=(P("seq", "tp"), P(None, "seq", "tp"), P(None, "tp"), P(None, "tp"), P("tp")),
        out_specs=P("seq", "tp"),
        check_vma=False,
    )
```

```python
import functools

import jax
import jax.numpy as jnp
from jax import lax
from jax.experimental import pallas as pl
from jax.experimental.pallas import tpu as pltpu
from jax.sharding import PartitionSpec as P

MESH = pl.DeviceIdType.MESH
RING = 4
CHIPS = RING * RING
CH = 128
WIDTHS = (256, 128, 128)
STARTS = (0, 256, 384)
SUBS = ((0, 1), (2,), (3,))
CHUNKS = len(WIDTHS)
HALF = sum(WIDTHS)
GROUPS = HALF // CH
TOK = 512
ROWS = 2 * TOK
FEAT = 1024
DEPTH = CHIPS * 256
FAR_FIRST = sorted(
    [(i, j) for i in range(RING) for j in range(RING) if i or j],
    key=lambda d: -sum(min(v, RING - v) for v in d),
)
SEGS = 8
SEG = TOK // SEGS


def sigmoid(v):
    return jax.nn.sigmoid(v)


def cell(pre, p, coef):
    u = sigmoid(pre[0] + coef[0] * p)
    r = sigmoid(pre[1] + coef[1] * p)
    c = jnp.tanh(pre[2] + coef[2] * r * p)
    keep = 1.0 - u
    slope = c - p
    jac = (
        keep
        + slope * (u * keep * coef[0])
        + u * ((1.0 - c * c) * coef[2]) * (r + p * (r * (1.0 - r) * coef[1]))
    )
    stepped = keep * p + u * c
    return jac, stepped - jac * p


def cell_at_zero(pre, coef):
    u = sigmoid(pre[0])
    r = sigmoid(pre[1])
    c = jnp.tanh(pre[2])
    keep = 1.0 - u
    jac = keep + c * (u * keep * coef[0]) + u * ((1.0 - c * c) * coef[2]) * r
    return jac, u * c


def kernel(
    tok_hbm, w_hbm, bias, rec, init, out,
    X, W0, W1, W2, PRE, AB1, AB2, OUTB, SEGT, MID, SUM, SLOT,
    local_sem, sib_s, sib_r, w_s, p1_r, p2_r, t_s, t_r, ts_s, ts_r, ex_s, ex_r, o_l, o_s, o_r,
):
    W = (W0, W1, W2)
    ORDER = (0, 3, 1, 2)
    seq, x = lax.axis_index("seq"), lax.axis_index("tp")
    c = lax.rem(seq, 2)
    q = seq // 2
    y, z = q // RING, lax.rem(q, RING)
    p = (1 - c) * y + c * z
    s = (1 - c) * z + c * y

    def block(pp, ss):
        return lax.rem(pp, RING) * (4 - 3 * c) + lax.rem(ss, RING) * (1 + 3 * c)

    def peer(qq):
        return (qq * 2 + c, x)

    right, left = peer(block(p + 1, s)), peer(block(p + 3, s))
    up, down = peer(block(p, s + 1)), peer(block(p, s + 3))
    xr, xl = (seq, lax.rem(x + 1, RING)), (seq, lax.rem(x + 3, RING))
    sib = (q * 2 + 1 - c, x)

    def rcopy(src, dst, ss, rs, dev):
        return pltpu.make_async_remote_copy(
            src_ref=src, dst_ref=dst, send_sem=ss, recv_sem=rs, device_id=dev, device_id_type=MESH
        )

    def send(ref, ss, rs, dev):
        rcopy(ref, ref, ss, rs, dev).start()

    def arrived(ref, sem):
        pltpu.make_async_copy(ref, ref, sem).wait()

    def wrows(k, blk, half=None):
        if half is None:
            return W[k].at[pl.ds(pl.multiple_of(blk * 256, 256), 256)]
        return W[k].at[pl.ds(pl.multiple_of(blk * 256 + half * 128, 128), 128)]

    def chan(core, k):
        return pl.ds(pl.multiple_of(core * HALF + STARTS[k], CH), WIDTHS[k])

    def lanes(core, sub):
        return pl.ds(pl.multiple_of(core * HALF + sub * CH, CH), CH)

    def trows(core, half=None):
        if half is None:
            return pl.ds(pl.multiple_of(core * TOK, TOK), TOK)
        return pl.ds(pl.multiple_of(core * TOK + half * 256, 256), 256)

    def tcols(xx):
        return pl.ds(pl.multiple_of(lax.rem(xx, RING) * FEAT, FEAT), FEAT)

    mine = pl.ds(pl.multiple_of(q * 256 + c * 128, 128), 128)
    own_tok = pltpu.make_async_copy(tok_hbm, X.at[trows(c), tcols(x)], local_sem.at[CHUNKS])
    for k in range(CHUNKS):
        for g in range(3):
            pltpu.make_async_copy(
                w_hbm.at[g, :, chan(c, k)],
                W[k].at[mine, pl.ds(g * WIDTHS[k], WIDTHS[k])],
                local_sem.at[k],
            ).start()
    own_tok.start()

    barrier = pltpu.get_barrier_semaphore()

    def greet(e, _):
        pl.semaphore_signal(
            barrier, inc=1, device_id=peer(lax.rem(q + e, CHIPS)), device_id_type=MESH
        )
        return 0

    lax.fori_loop(1, CHIPS, greet, 0)
    for d in (xr, xl, sib):
        pl.semaphore_signal(barrier, inc=1, device_id=d, device_id_type=MESH)
    pl.semaphore_wait(barrier, CHIPS + 2)

    for k in range(CHUNKS):
        for g in range(3):
            rcopy(
                w_hbm.at[g, :, chan(1 - c, k)],
                W[k].at[mine, pl.ds(g * WIDTHS[k], WIDTHS[k])],
                sib_s.at[k], sib_r.at[k], sib,
            ).start()
        arrived(wrows(k, q, c), local_sem.at[k])
        send(wrows(k, q, c), w_s.at[k], p1_r.at[k, 0], right)
        send(wrows(k, q, c), w_s.at[k], p1_r.at[k, 1], left)
    own_tok.wait()
    for h in range(2):
        send(X.at[trows(c, h), tcols(x)], t_s.at[0, h], t_r.at[0, h], xr)
        send(X.at[trows(c, 1 - h), tcols(x)], t_s.at[1, 1 - h], t_r.at[1, 1 - h], xl)
    send(X.at[trows(c), tcols(x)], ts_s.at[0], ts_r.at[0], sib)

    def send2(k, i):
        own = block(p + i, s)
        send(wrows(k, own, 0), w_s.at[k], p2_r.at[k, i, 0], up)
        send(wrows(k, own, 1), w_s.at[k], p2_r.at[k, i, 1], down)

    def send2b(k, i):
        own = block(p + i, s)
        send(wrows(k, own, 1), w_s.at[k], p2_r.at[k, i, 4], up)
        send(wrows(k, own, 0), w_s.at[k], p2_r.at[k, i, 5], down)

    def sibling_rows(k):
        arrived(wrows(k, q, 1 - c), sib_r.at[k])
        send(wrows(k, q, 1 - c), w_s.at[k], p1_r.at[k, 2], right)
        send(wrows(k, q, 1 - c), w_s.at[k], p1_r.at[k, 3], left)

    def ring_on(k):
        arrived(wrows(k, block(p + 3, s), c), p1_r.at[k, 0])
        send(wrows(k, block(p + 3, s), c), w_s.at[k], p1_r.at[k, 4], right)
        arrived(wrows(k, block(p + 1, s), c), p1_r.at[k, 1])
        arrived(wrows(k, block(p + 1, s), 1 - c), p1_r.at[k, 3])
        send(wrows(k, block(p + 1, s), 1 - c), w_s.at[k], p1_r.at[k, 5], left)
        arrived(wrows(k, block(p + 3, s), 1 - c), p1_r.at[k, 2])

    def ring_end(k):
        arrived(wrows(k, block(p + 2, s), c), p1_r.at[k, 4])
        arrived(wrows(k, block(p + 2, s), 1 - c), p1_r.at[k, 5])

    def pass_on(k, i):
        below, above = block(p + i, s + 3), block(p + i, s + 1)
        arrived(wrows(k, below, 0), p2_r.at[k, i, 0])
        send(wrows(k, below, 0), w_s.at[k], p2_r.at[k, i, 2], up)
        arrived(wrows(k, above, 1), p2_r.at[k, i, 1])
        send(wrows(k, above, 1), w_s.at[k], p2_r.at[k, i, 3], down)

    def near(k, i):
        arrived(wrows(k, block(p + i, s + 3), 1), p2_r.at[k, i, 4])
        arrived(wrows(k, block(p + i, s + 1), 0), p2_r.at[k, i, 5])

    def far(k, i):
        for h in range(2):
            arrived(wrows(k, block(p + i, s + 2), h), p2_r.at[k, i, 2 + h])

    def gathered(k):
        for i in ORDER:
            near(k, i)
            far(k, i)

    def features_first():
        arrived(X.at[trows(c, 0), tcols(x + 3)], t_r.at[0, 0])
        send(X.at[trows(c, 0), tcols(x + 3)], t_s.at[2, 0], t_r.at[2, 0], xr)
        arrived(X.at[trows(c, 1), tcols(x + 1)], t_r.at[1, 1])
        send(X.at[trows(c, 1), tcols(x + 1)], t_s.at[2, 1], t_r.at[2, 1], xl)
        send(X.at[trows(c, 0), tcols(x + 3)], ts_s.at[1], ts_r.at[1], sib)
        send(X.at[trows(c, 1), tcols(x + 1)], ts_s.at[2], ts_r.at[2], sib)

    def features_second():
        arrived(X.at[trows(c, 1), tcols(x + 3)], t_r.at[0, 1])
        send(X.at[trows(c, 1), tcols(x + 3)], ts_s.at[3], ts_r.at[3], sib)
        arrived(X.at[trows(c, 0), tcols(x + 1)], t_r.at[1, 0])
        send(X.at[trows(c, 0), tcols(x + 1)], ts_s.at[4], ts_r.at[4], sib)

    def features_end():
        for h in range(2):
            arrived(X.at[trows(c, h), tcols(x + 2)], t_r.at[2, h])
            send(X.at[trows(c, h), tcols(x + 2)], ts_s.at[5 + h], ts_r.at[5 + h], sib)
        arrived(X.at[trows(1 - c), tcols(x)], ts_r.at[0])
        for n, (h, d) in enumerate(((0, 3), (1, 1), (1, 3), (0, 1), (0, 2), (1, 2))):
            arrived(X.at[trows(1 - c, h), tcols(x + d)], ts_r.at[1 + n])

    def row_of(ref, g, sub):
        return ref[pl.ds(g, 1), lanes(c, sub)]

    def put(k, acc, t, add):
        m = c if t < 2 else 1 - c
        for n, sub in enumerate(SUBS[k]):
            for g in range(3):
                v = acc[:, g * WIDTHS[k] + n * CH : g * WIDTHS[k] + (n + 1) * CH]
                if not add:
                    v = v + row_of(bias, g, sub)
                for h in range(SEGS // 2):
                    at = pl.ds((t % 2) * (SEGS // 2) + h, SEG, stride=SEGS)
                    part = v[h * SEG : (h + 1) * SEG]
                    PRE[sub, g, m, at, :] = PRE[sub, g, m, at, :] + part if add else part

    def quarter(t):
        return trows(c if t < 2 else 1 - c, t % 2)

    def matmul(k, t):
        acc = jnp.dot(X[quarter(t), :], W[k][...], preferred_element_type=jnp.float32)
        put(k, acc, t, False)

    def matmul_part(k, t, places, add):
        at = [
            pl.ds(pl.multiple_of(block(p + i, s + o) * 256, 256), 256)
            for i in places
            for o in range(RING)
        ]
        a = jnp.concatenate([X[quarter(t), d] for d in at], axis=1)
        b = jnp.concatenate([W[k][d, :] for d in at], axis=0)
        put(k, jnp.dot(a, b, preferred_element_type=jnp.float32), t, add)

    def vreg(j):
        return pl.ds(pl.multiple_of(j * SEGS, SEGS), SEGS)

    sublane = lax.broadcasted_iota(jnp.int32, (SEGS, CH), 0)

    def coefs(sub):
        return [jnp.broadcast_to(row_of(rec, g, sub), (SEGS, CH)) for g in range(3)]

    def publish(n, sub, AB):
        tot = []
        for m in range(2):
            SEGT[n, sub, m, 0], SEGT[n, sub, m, 1] = AB[m]
            ta, tb = SEGT[n, sub, m, 0, 0:1], SEGT[n, sub, m, 1, 0:1]
            for i in range(1, SEGS):
                a, b = SEGT[n, sub, m, 0, i : i + 1], SEGT[n, sub, m, 1, i : i + 1]
                ta, tb = a * ta, a * tb + b
            tot.append((ta, tb))
        (a0, b0), (a1, b1) = tot
        MID[n, sub] = jnp.where(sublane == 0, a0, b0)
        SUM[n, sub] = jnp.where(sublane == 0, a0 * a1, a1 * b0 + b1)

    def span(k):
        return pl.ds(SUBS[k][0], len(SUBS[k]))

    def exchange(n, k):
        for dy, dz in FAR_FIRST:
            there = lax.rem(y + dy, RING) * RING + lax.rem(z + dz, RING)
            rcopy(
                SUM.at[n, span(k)], SLOT.at[n, lax.rem(there - q + CHIPS, CHIPS), span(k)],
                ex_s.at[n, k], ex_r.at[n, k], peer(there),
            ).start()

    def exchanged(n, k, sem):
        arrived(SLOT.at[n, pl.ds(1, CHIPS - 1), span(k)], sem.at[n, k])

    def incoming(n, sub):
        h = row_of(init, 0, sub)
        for e in range(CHIPS - 1, 0, -1):
            h = jnp.where(e <= q, SLOT[n, e, sub, 0:1] * h + SLOT[n, e, sub, 1:2], h)
        starts = [h, MID[n, sub, 0:1] * h + MID[n, sub, 1:2]]
        for m in range(2):
            h = starts[m]
            SEGT[n, sub, m, 2, 0:1] = h
            for i in range(SEGS - 1):
                h = SEGT[n, sub, m, 0, i : i + 1] * h + SEGT[n, sub, m, 1, i : i + 1]
                SEGT[n, sub, m, 2, i + 1 : i + 2] = h
        return [SEGT[n, sub, m, 2] for m in range(2)]

    UN = 4

    def pass1(sub):
        coef = coefs(sub)
        first = (sublane + q) == 0
        p0 = jnp.where(first, jnp.broadcast_to(row_of(init, 0, sub), (SEGS, CH)), 0.0)

        def step(j, AB, p0=None):
            new = []
            for m in range(2):
                v = vreg(j)
                pre = [PRE[sub, g, m, v, :] for g in range(3)]
                a, b = cell_at_zero(pre, coef) if p0 is None or m else cell(pre, p0, coef)
                AB1[sub, 0, m, v, :] = a
                AB1[sub, 1, m, v, :] = b
                new.append((a, b) if AB is None else (a * AB[m][0], a * AB[m][1] + b))
            return new

        AB = step(0, None, p0)
        for j in range(1, UN):
            AB = step(j, AB)

        def group(t, AB):
            for o in range(UN):
                AB = step(t * UN + o, AB)
            return AB

        publish(0, sub, lax.fori_loop(1, SEG // UN, group, AB))

    def pass2(sub):
        coef = coefs(sub)

        def group(t, carry):
            for o in range(UN):
                v = vreg(t * UN + o)
                new = []
                for m in range(2):
                    h, A, B = carry[m]
                    a, b = cell([PRE[sub, g, m, v, :] for g in range(3)], h, coef)
                    AB2[sub, 0, m, v, :] = a
                    AB2[sub, 1, m, v, :] = b
                    h = AB1[sub, 0, m, v, :] * h + AB1[sub, 1, m, v, :]
                    new.append((h, a * A, a * B + b))
                carry = new
            return carry

        one, zero = jnp.ones((SEGS, CH), jnp.float32), jnp.zeros((SEGS, CH), jnp.float32)
        carry = lax.fori_loop(0, SEG // UN, group, [(h, one, zero) for h in incoming(0, sub)])
        publish(1, sub, [(A, B) for _, A, B in carry])

    def pass3(sub):
        def group(t, hs):
            for o in range(UN):
                j = t * UN + o
                v = vreg(j)
                hs = [AB2[sub, 0, m, v, :] * hs[m] + AB2[sub, 1, m, v, :] for m in range(2)]
                for m in range(2):
                    OUTB[sub, pl.ds(m * TOK + j, SEGS, stride=SEG), :] = hs[m]
            return hs

        lax.fori_loop(0, SEG // UN, group, incoming(1, sub))
        here = out.at[:, lanes(c, sub)]
        rcopy(OUTB.at[sub, trows(1 - c)], here, o_s.at[sub], o_r.at[sub], sib).start()
        pltpu.make_async_copy(OUTB.at[sub, trows(c)], here, o_l.at[sub]).start()

    def put_out(sub):
        here, there = out.at[:, lanes(c, sub)], out.at[:, lanes(1 - c, sub)]
        arrived(here, o_l.at[sub])
        arrived(here, o_s.at[sub])
        arrived(there, o_r.at[sub])

    def first_pass(k):
        for sub in SUBS[k]:
            pass1(sub)
        exchange(0, k)

    def second_pass(k, between=()):
        exchanged(0, k, ex_r)
        for n, sub in enumerate(SUBS[k]):
            pass2(sub)
            if n < len(between):
                pass_on(2, between[n])
        exchange(1, k)

    def last_pass(k):
        exchanged(1, k, ex_r)
        for sub in SUBS[k]:
            pass3(sub)

    def sent(k):
        arrived(wrows(k, q, c), sib_s.at[k])
        arrived(W[k].at[pl.ds(0, 30 * 128)], w_s.at[k])

    def sent_features():
        for h in range(2):
            for d in range(3):
                arrived(X.at[trows(c, h), tcols(x)], t_s.at[d, h])
        arrived(X.at[trows(c), tcols(x)], ts_s.at[0])
        for n in range(6):
            arrived(X.at[trows(c, 0), tcols(x)], ts_s.at[1 + n])

    for k in range(CHUNKS):
        sibling_rows(k)
        if k == 0:
            send2(0, 0)
    for k in range(CHUNKS):
        ring_on(k)
        if k == 0:
            send2(0, 3)
            send2(0, 1)
            send2b(0, 0)
    features_first()
    ring_end(0)
    send2(0, 2)
    ring_end(1)
    ring_end(2)
    send2b(0, 3)
    send2b(0, 1)
    send2b(0, 2)
    pass_on(0, 0)
    pass_on(0, 3)
    send2(1, 0)
    features_second()
    pass_on(0, 1)
    send2(1, 3)
    pass_on(0, 2)
    send2(1, 1)
    send2(1, 2)
    for i in ORDER:
        send2b(1, i)
    features_end()
    gathered(0)
    send2(2, 0)
    send2b(2, 0)
    for t in range(4):
        matmul(0, t)
        pass_on(1, ORDER[t])
        if t == 2:
            send2(2, 3)
            send2b(2, 3)
    for i in (1, 2):
        send2(2, i)
        send2b(2, i)
    first_pass(0)
    pass_on(2, 0)
    gathered(1)
    for t in range(4):
        matmul(1, t)
        if t == 1:
            pass_on(2, 3)
    pass_on(2, 1)
    first_pass(1)
    second_pass(0, (2,))
    for i in (0, 3, 1):
        near(2, i)
        far(2, i)
    for t in range(4):
        matmul_part(2, t, (0, 3, 1), False)
    second_pass(1)
    sent(0)
    sent(1)
    sent_features()
    near(2, 2)
    far(2, 2)
    for t in range(4):
        matmul_part(2, t, (2,), True)
    first_pass(2)
    last_pass(0)
    last_pass(1)
    sent(2)
    for k in range(CHUNKS - 1):
        exchanged(0, k, ex_s)
        exchanged(1, k, ex_s)
    second_pass(2)
    for k in range(CHUNKS - 1):
        for sub in SUBS[k]:
            put_out(sub)
    exchanged(0, 2, ex_s)
    last_pass(2)
    exchanged(1, 2, ex_s)
    put_out(SUBS[2][0])


def body(tokens, weights, gate_bias, recurrent, initial_state):
    dma = pltpu.SemaphoreType.DMA
    f32, bf16 = jnp.float32, jnp.bfloat16
    vmem, hbm = pl.BlockSpec(memory_space=pltpu.VMEM), pl.BlockSpec(memory_space=pl.ANY)
    return pl.pallas_call(
        kernel,
        out_shape=jax.ShapeDtypeStruct((TOK, 2 * HALF), f32),
        in_specs=[hbm, hbm, vmem, vmem, vmem],
        out_specs=hbm,
        scratch_shapes=[
            pltpu.VMEM((ROWS, DEPTH), bf16),
            *[pltpu.VMEM((DEPTH, 3 * w), bf16) for w in WIDTHS],
            pltpu.VMEM((GROUPS, 3, 2, TOK, CH), f32),
            pltpu.VMEM((GROUPS, 2, 2, TOK, CH), f32),
            pltpu.VMEM((GROUPS, 2, 2, TOK, CH), f32),
            pltpu.VMEM((GROUPS, ROWS, CH), f32),
            pltpu.VMEM((2, GROUPS, 2, 3, SEGS, CH), f32),
            pltpu.VMEM((2, GROUPS, SEGS, CH), f32),
            pltpu.VMEM((2, GROUPS, SEGS, CH), f32),
            pltpu.VMEM((2, CHIPS, GROUPS, SEGS, CH), f32),
            dma((CHUNKS + 1,)),
            dma((CHUNKS,)),
            dma((CHUNKS,)),
            dma((CHUNKS,)),
            dma((CHUNKS, 6)),
            dma((CHUNKS, RING, 6)),
            dma((3, 2)),
            dma((3, 2)),
            dma((7,)),
            dma((7,)),
            dma((2, CHUNKS)),
            dma((2, CHUNKS)),
            dma((GROUPS,)),
            dma((GROUPS,)),
            dma((GROUPS,)),
        ],
        compiler_params=pltpu.CompilerParams(
            collective_id=0, has_side_effects=True, vmem_limit_bytes=56 * 2**20
        ),
        cost_estimate=pl.CostEstimate(
            flops=2 * ROWS * DEPTH * 3 * HALF, bytes_accessed=8 * 2**20, transcendentals=0
        ),
    )(tokens, weights, gate_bias, recurrent, initial_state[None, :])


def solution(mesh):
    return jax.shard_map(
        body,
        mesh=mesh,
        in_specs=(P("seq", "tp"), P(None, "seq", "tp"), P(None, "tp"), P(None, "tp"), P("tp")),
        out_specs=P("seq", "tp"),
        check_vma=False,
    )
```

```python
import functools

import jax
import jax.numpy as jnp
from jax import lax
from jax.experimental import pallas as pl
from jax.experimental.pallas import tpu as pltpu
from jax.sharding import PartitionSpec as P

MESH = pl.DeviceIdType.MESH
RING = 4
CHIPS = RING * RING
CH = 128
WIDTHS = (256, 128, 128)
STARTS = (0, 256, 384)
SUBS = ((0, 1), (2,), (3,))
CHUNKS = len(WIDTHS)
HALF = sum(WIDTHS)
GROUPS = HALF // CH
TOK = 512
ROWS = 2 * TOK
FEAT = 1024
DEPTH = CHIPS * 256
FAR_FIRST = sorted(
    [(i, j) for i in range(RING) for j in range(RING) if i or j],
    key=lambda d: -sum(min(v, RING - v) for v in d),
)
SEGS = 8
SEG = TOK // SEGS


def sigmoid(v):
    return jax.nn.sigmoid(v)


def cell(pre, p, coef):
    u = sigmoid(pre[0] + coef[0] * p)
    r = sigmoid(pre[1] + coef[1] * p)
    c = jnp.tanh(pre[2] + coef[2] * r * p)
    keep = 1.0 - u
    slope = c - p
    jac = (
        keep
        + slope * (u * keep * coef[0])
        + u * ((1.0 - c * c) * coef[2]) * (r + p * (r * (1.0 - r) * coef[1]))
    )
    stepped = keep * p + u * c
    return jac, stepped - jac * p


def cell_at_zero(pre, coef):
    u = sigmoid(pre[0])
    r = sigmoid(pre[1])
    c = jnp.tanh(pre[2])
    keep = 1.0 - u
    jac = keep + c * (u * keep * coef[0]) + u * ((1.0 - c * c) * coef[2]) * r
    return jac, u * c


def kernel(
    tok_hbm, w_hbm, bias, rec, init, out,
    X, W0, W1, W2, PRE, AB1, AB2, OUTB, SEGT, MID, SUM, SLOT,
    local_sem, sib_s, sib_r, w_s, p1_r, p2_r, t_s, t_r, ts_s, ts_r, ex_s, ex_r, o_l, o_s, o_r,
):
    W = (W0, W1, W2)
    ORDER = (0, 3, 1, 2)
    seq, x = lax.axis_index("seq"), lax.axis_index("tp")
    c = lax.rem(seq, 2)
    q = seq // 2
    y, z = q // RING, lax.rem(q, RING)
    p = (1 - c) * y + c * z
    s = (1 - c) * z + c * y

    def block(pp, ss):
        return lax.rem(pp, RING) * (4 - 3 * c) + lax.rem(ss, RING) * (1 + 3 * c)

    def peer(qq):
        return (qq * 2 + c, x)

    right, left = peer(block(p + 1, s)), peer(block(p + 3, s))
    up, down = peer(block(p, s + 1)), peer(block(p, s + 3))
    xr, xl = (seq, lax.rem(x + 1, RING)), (seq, lax.rem(x + 3, RING))
    sib = (q * 2 + 1 - c, x)

    def rcopy(src, dst, ss, rs, dev):
        return pltpu.make_async_remote_copy(
            src_ref=src, dst_ref=dst, send_sem=ss, recv_sem=rs, device_id=dev, device_id_type=MESH
        )

    def send(ref, ss, rs, dev):
        rcopy(ref, ref, ss, rs, dev).start()

    def arrived(ref, sem):
        pltpu.make_async_copy(ref, ref, sem).wait()

    def wrows(k, blk, half=None):
        if half is None:
            return W[k].at[pl.ds(pl.multiple_of(blk * 256, 256), 256)]
        return W[k].at[pl.ds(pl.multiple_of(blk * 256 + half * 128, 128), 128)]

    def chan(core, k):
        return pl.ds(pl.multiple_of(core * HALF + STARTS[k], CH), WIDTHS[k])

    def lanes(core, sub):
        return pl.ds(pl.multiple_of(core * HALF + sub * CH, CH), CH)

    def trows(core, half=None):
        if half is None:
            return pl.ds(pl.multiple_of(core * TOK, TOK), TOK)
        return pl.ds(pl.multiple_of(core * TOK + half * 256, 256), 256)

    def tcols(xx):
        return pl.ds(pl.multiple_of(lax.rem(xx, RING) * FEAT, FEAT), FEAT)

    mine = pl.ds(pl.multiple_of(q * 256 + c * 128, 128), 128)
    own_tok = pltpu.make_async_copy(tok_hbm, X.at[trows(c), tcols(x)], local_sem.at[CHUNKS])
    for k in range(CHUNKS):
        for g in range(3):
            pltpu.make_async_copy(
                w_hbm.at[g, :, chan(c, k)],
                W[k].at[mine, pl.ds(g * WIDTHS[k], WIDTHS[k])],
                local_sem.at[k],
            ).start()
    own_tok.start()

    barrier = pltpu.get_barrier_semaphore()

    for d in (right, left, up, down, xr, xl, sib):
        pl.semaphore_signal(barrier, inc=1, device_id=d, device_id_type=MESH)
    pl.semaphore_wait(barrier, 7)

    for k in range(CHUNKS):
        for g in range(3):
            rcopy(
                w_hbm.at[g, :, chan(1 - c, k)],
                W[k].at[mine, pl.ds(g * WIDTHS[k], WIDTHS[k])],
                sib_s.at[k], sib_r.at[k], sib,
            ).start()
        arrived(wrows(k, q, c), local_sem.at[k])
        send(wrows(k, q, c), w_s.at[k], p1_r.at[k, 0], right)
        send(wrows(k, q, c), w_s.at[k], p1_r.at[k, 1], left)
    own_tok.wait()
    for h in range(2):
        send(X.at[trows(c, h), tcols(x)], t_s.at[0, h], t_r.at[0, h], xr)
        send(X.at[trows(c, 1 - h), tcols(x)], t_s.at[1, 1 - h], t_r.at[1, 1 - h], xl)
    send(X.at[trows(c), tcols(x)], ts_s.at[0], ts_r.at[0], sib)

    def send2(k, i):
        own = block(p + i, s)
        send(wrows(k, own, 0), w_s.at[k], p2_r.at[k, i, 0], up)
        send(wrows(k, own, 1), w_s.at[k], p2_r.at[k, i, 1], down)

    def send2b(k, i):
        own = block(p + i, s)
        send(wrows(k, own, 1), w_s.at[k], p2_r.at[k, i, 4], up)
        send(wrows(k, own, 0), w_s.at[k], p2_r.at[k, i, 5], down)

    def sibling_rows(k):
        arrived(wrows(k, q, 1 - c), sib_r.at[k])
        send(wrows(k, q, 1 - c), w_s.at[k], p1_r.at[k, 2], right)
        send(wrows(k, q, 1 - c), w_s.at[k], p1_r.at[k, 3], left)

    def ring_on(k):
        arrived(wrows(k, block(p + 3, s), c), p1_r.at[k, 0])
        send(wrows(k, block(p + 3, s), c), w_s.at[k], p1_r.at[k, 4], right)
        arrived(wrows(k, block(p + 1, s), c), p1_r.at[k, 1])
        arrived(wrows(k, block(p + 1, s), 1 - c), p1_r.at[k, 3])
        send(wrows(k, block(p + 1, s), 1 - c), w_s.at[k], p1_r.at[k, 5], left)
        arrived(wrows(k, block(p + 3, s), 1 - c), p1_r.at[k, 2])

    def ring_end(k):
        arrived(wrows(k, block(p + 2, s), c), p1_r.at[k, 4])
        arrived(wrows(k, block(p + 2, s), 1 - c), p1_r.at[k, 5])

    def pass_on(k, i):
        below, above = block(p + i, s + 3), block(p + i, s + 1)
        arrived(wrows(k, below, 0), p2_r.at[k, i, 0])
        send(wrows(k, below, 0), w_s.at[k], p2_r.at[k, i, 2], up)
        arrived(wrows(k, above, 1), p2_r.at[k, i, 1])
        send(wrows(k, above, 1), w_s.at[k], p2_r.at[k, i, 3], down)

    def near(k, i):
        arrived(wrows(k, block(p + i, s + 3), 1), p2_r.at[k, i, 4])
        arrived(wrows(k, block(p + i, s + 1), 0), p2_r.at[k, i, 5])

    def far(k, i):
        for h in range(2):
            arrived(wrows(k, block(p + i, s + 2), h), p2_r.at[k, i, 2 + h])

    def gathered(k):
        for i in ORDER:
            near(k, i)
            far(k, i)

    def features_first():
        arrived(X.at[trows(c, 0), tcols(x + 3)], t_r.at[0, 0])
        send(X.at[trows(c, 0), tcols(x + 3)], t_s.at[2, 0], t_r.at[2, 0], xr)
        arrived(X.at[trows(c, 1), tcols(x + 1)], t_r.at[1, 1])
        send(X.at[trows(c, 1), tcols(x + 1)], t_s.at[2, 1], t_r.at[2, 1], xl)
        send(X.at[trows(c, 0), tcols(x + 3)], ts_s.at[1], ts_r.at[1], sib)
        send(X.at[trows(c, 1), tcols(x + 1)], ts_s.at[2], ts_r.at[2], sib)

    def features_second():
        arrived(X.at[trows(c, 1), tcols(x + 3)], t_r.at[0, 1])
        send(X.at[trows(c, 1), tcols(x + 3)], ts_s.at[3], ts_r.at[3], sib)
        arrived(X.at[trows(c, 0), tcols(x + 1)], t_r.at[1, 0])
        send(X.at[trows(c, 0), tcols(x + 1)], ts_s.at[4], ts_r.at[4], sib)

    def features_end():
        for h in range(2):
            arrived(X.at[trows(c, h), tcols(x + 2)], t_r.at[2, h])
            send(X.at[trows(c, h), tcols(x + 2)], ts_s.at[5 + h], ts_r.at[5 + h], sib)
        arrived(X.at[trows(1 - c), tcols(x)], ts_r.at[0])
        for n, (h, d) in enumerate(((0, 3), (1, 1), (1, 3), (0, 1), (0, 2), (1, 2))):
            arrived(X.at[trows(1 - c, h), tcols(x + d)], ts_r.at[1 + n])

    def row_of(ref, g, sub):
        return ref[pl.ds(g, 1), lanes(c, sub)]

    def put(k, acc, t, add):
        m = c if t < 2 else 1 - c
        for n, sub in enumerate(SUBS[k]):
            for g in range(3):
                v = acc[:, g * WIDTHS[k] + n * CH : g * WIDTHS[k] + (n + 1) * CH]
                if not add:
                    v = v + row_of(bias, g, sub)
                for h in range(SEGS // 2):
                    at = pl.ds((t % 2) * (SEGS // 2) + h, SEG, stride=SEGS)
                    part = v[h * SEG : (h + 1) * SEG]
                    PRE[sub, g, m, at, :] = PRE[sub, g, m, at, :] + part if add else part

    def quarter(t):
        return trows(c if t < 2 else 1 - c, t % 2)

    def matmul(k, t):
        acc = jnp.dot(X[quarter(t), :], W[k][...], preferred_element_type=jnp.float32)
        put(k, acc, t, False)

    def matmul_part(k, t, chips, add):
        at = [pl.ds(pl.multiple_of(block(p + i, s + o) * 256, 256), 256) for i, o in chips]
        a = jnp.concatenate([X[quarter(t), d] for d in at], axis=1)
        b = jnp.concatenate([W[k][d, :] for d in at], axis=0)
        put(k, jnp.dot(a, b, preferred_element_type=jnp.float32), t, add)

    def vreg(j):
        return pl.ds(pl.multiple_of(j * SEGS, SEGS), SEGS)

    sublane = lax.broadcasted_iota(jnp.int32, (SEGS, CH), 0)

    def coefs(sub):
        return [jnp.broadcast_to(row_of(rec, g, sub), (SEGS, CH)) for g in range(3)]

    def publish(n, sub, AB):
        tot = []
        for m in range(2):
            SEGT[n, sub, m, 0], SEGT[n, sub, m, 1] = AB[m]
            ta, tb = SEGT[n, sub, m, 0, 0:1], SEGT[n, sub, m, 1, 0:1]
            for i in range(1, SEGS):
                a, b = SEGT[n, sub, m, 0, i : i + 1], SEGT[n, sub, m, 1, i : i + 1]
                ta, tb = a * ta, a * tb + b
            tot.append((ta, tb))
        (a0, b0), (a1, b1) = tot
        MID[n, sub] = jnp.where(sublane == 0, a0, b0)
        SUM[n, sub] = jnp.where(sublane == 0, a0 * a1, a1 * b0 + b1)

    def span(k):
        return pl.ds(SUBS[k][0], len(SUBS[k]))

    def exchange(n, k):
        for dy, dz in FAR_FIRST:
            there = lax.rem(y + dy, RING) * RING + lax.rem(z + dz, RING)
            rcopy(
                SUM.at[n, span(k)], SLOT.at[n, lax.rem(there - q + CHIPS, CHIPS), span(k)],
                ex_s.at[n, k], ex_r.at[n, k], peer(there),
            ).start()

    def exchanged(n, k, sem):
        arrived(SLOT.at[n, pl.ds(1, CHIPS - 1), span(k)], sem.at[n, k])

    def incoming(n, sub):
        h = row_of(init, 0, sub)
        for e in range(CHIPS - 1, 0, -1):
            h = jnp.where(e <= q, SLOT[n, e, sub, 0:1] * h + SLOT[n, e, sub, 1:2], h)
        starts = [h, MID[n, sub, 0:1] * h + MID[n, sub, 1:2]]
        for m in range(2):
            h = starts[m]
            SEGT[n, sub, m, 2, 0:1] = h
            for i in range(SEGS - 1):
                h = SEGT[n, sub, m, 0, i : i + 1] * h + SEGT[n, sub, m, 1, i : i + 1]
                SEGT[n, sub, m, 2, i + 1 : i + 2] = h
        return [SEGT[n, sub, m, 2] for m in range(2)]

    UN = 4

    def pass1(sub):
        coef = coefs(sub)
        first = (sublane + q) == 0
        p0 = jnp.where(first, jnp.broadcast_to(row_of(init, 0, sub), (SEGS, CH)), 0.0)

        def step(j, AB, p0=None):
            new = []
            for m in range(2):
                v = vreg(j)
                pre = [PRE[sub, g, m, v, :] for g in range(3)]
                a, b = cell_at_zero(pre, coef) if p0 is None or m else cell(pre, p0, coef)
                AB1[sub, 0, m, v, :] = a
                AB1[sub, 1, m, v, :] = b
                new.append((a, b) if AB is None else (a * AB[m][0], a * AB[m][1] + b))
            return new

        AB = step(0, None, p0)
        for j in range(1, UN):
            AB = step(j, AB)

        def group(t, AB):
            for o in range(UN):
                AB = step(t * UN + o, AB)
            return AB

        publish(0, sub, lax.fori_loop(1, SEG // UN, group, AB))

    def pass2(sub):
        coef = coefs(sub)

        def group(t, carry):
            for o in range(UN):
                v = vreg(t * UN + o)
                new = []
                for m in range(2):
                    h, A, B = carry[m]
                    a, b = cell([PRE[sub, g, m, v, :] for g in range(3)], h, coef)
                    AB2[sub, 0, m, v, :] = a
                    AB2[sub, 1, m, v, :] = b
                    h = AB1[sub, 0, m, v, :] * h + AB1[sub, 1, m, v, :]
                    new.append((h, a * A, a * B + b))
                carry = new
            return carry

        one, zero = jnp.ones((SEGS, CH), jnp.float32), jnp.zeros((SEGS, CH), jnp.float32)
        carry = lax.fori_loop(0, SEG // UN, group, [(h, one, zero) for h in incoming(0, sub)])
        publish(1, sub, [(A, B) for _, A, B in carry])

    def pass3(sub):
        def group(t, hs):
            for o in range(UN):
                j = t * UN + o
                v = vreg(j)
                hs = [AB2[sub, 0, m, v, :] * hs[m] + AB2[sub, 1, m, v, :] for m in range(2)]
                for m in range(2):
                    OUTB[sub, pl.ds(m * TOK + j, SEGS, stride=SEG), :] = hs[m]
            return hs

        lax.fori_loop(0, SEG // UN, group, incoming(1, sub))
        here = out.at[:, lanes(c, sub)]
        rcopy(OUTB.at[sub, trows(1 - c)], here, o_s.at[sub], o_r.at[sub], sib).start()
        pltpu.make_async_copy(OUTB.at[sub, trows(c)], here, o_l.at[sub]).start()

    def put_out(sub):
        here, there = out.at[:, lanes(c, sub)], out.at[:, lanes(1 - c, sub)]
        arrived(here, o_l.at[sub])
        arrived(here, o_s.at[sub])
        arrived(there, o_r.at[sub])

    def first_pass(k):
        for sub in SUBS[k]:
            pass1(sub)
        exchange(0, k)

    def second_pass(k, between=()):
        exchanged(0, k, ex_r)
        for n, sub in enumerate(SUBS[k]):
            pass2(sub)
            if n < len(between):
                pass_on(2, between[n])
        exchange(1, k)

    def last_pass(k):
        exchanged(1, k, ex_r)
        for sub in SUBS[k]:
            pass3(sub)

    def sent(k):
        arrived(wrows(k, q, c), sib_s.at[k])
        arrived(W[k].at[pl.ds(0, 30 * 128)], w_s.at[k])

    def sent_features():
        for h in range(2):
            for d in range(3):
                arrived(X.at[trows(c, h), tcols(x)], t_s.at[d, h])
        arrived(X.at[trows(c), tcols(x)], ts_s.at[0])
        for n in range(6):
            arrived(X.at[trows(c, 0), tcols(x)], ts_s.at[1 + n])

    for k in range(CHUNKS):
        sibling_rows(k)
        if k == 0:
            send2(0, 0)
    for k in range(CHUNKS):
        ring_on(k)
        if k == 0:
            send2(0, 3)
            send2(0, 1)
            send2b(0, 0)
    features_first()
    ring_end(0)
    send2(0, 2)
    ring_end(1)
    ring_end(2)
    send2b(0, 3)
    send2b(0, 1)
    send2b(0, 2)
    pass_on(0, 0)
    pass_on(0, 3)
    send2(1, 0)
    features_second()
    pass_on(0, 1)
    send2(1, 3)
    pass_on(0, 2)
    send2(1, 1)
    send2(1, 2)
    for i in ORDER:
        send2b(1, i)
    features_end()
    gathered(0)
    send2(2, 0)
    send2b(2, 0)
    for t in range(4):
        matmul(0, t)
        pass_on(1, ORDER[t])
        if t == 2:
            send2(2, 3)
            send2b(2, 3)
    for i in (1, 2):
        send2(2, i)
        send2b(2, i)
    first_pass(0)
    for i in ORDER:
        near(1, i)
    for t in range(4):
        matmul_part(1, t, [(i, o) for o in (0, 1, 3) for i in ORDER], False)
        if t % 2 == 1:
            pass_on(2, ORDER[t // 2])
    for i in ORDER:
        far(1, i)
    for t in range(4):
        matmul_part(1, t, [(i, 2) for i in ORDER], True)
    first_pass(1)
    pass_on(2, 1)
    second_pass(0, (2,))
    for i in ORDER:
        near(2, i)
    for t in range(4):
        matmul_part(2, t, [(i, o) for o in (0, 1, 3) for i in ORDER], False)
    far(2, 0)
    far(2, 3)
    for t in range(4):
        matmul_part(2, t, [(i, 2) for i in (0, 3)], True)
    far(2, 1)
    far(2, 2)
    for t in range(4):
        matmul_part(2, t, [(i, 2) for i in (1, 2)], True)
    first_pass(2)
    second_pass(1)
    last_pass(0)
    sent(0)
    sent(1)
    second_pass(2)
    last_pass(1)
    sent(2)
    sent_features()
    for k in range(CHUNKS):
        exchanged(0, k, ex_s)
    exchanged(1, 0, ex_s)
    exchanged(1, 1, ex_s)
    for k in range(CHUNKS - 1):
        for sub in SUBS[k]:
            put_out(sub)
    last_pass(2)
    exchanged(1, 2, ex_s)
    put_out(SUBS[2][0])


def copy_out(src, dst, buf, load, store):
    rows = TOK // 8
    ins = [
        pltpu.make_async_copy(src.at[pl.ds(i * rows, rows)], buf.at[pl.ds(i * rows, rows)], load.at[i])
        for i in range(8)
    ]
    outs = [
        pltpu.make_async_copy(buf.at[pl.ds(i * rows, rows)], dst.at[pl.ds(i * rows, rows)], store.at[i])
        for i in range(8)
    ]
    for cp in ins:
        cp.start()
    for cp, nxt in zip(ins, outs):
        cp.wait()
        nxt.start()
    for cp in outs:
        cp.wait()


def body(tokens, weights, gate_bias, recurrent, initial_state):
    dma = pltpu.SemaphoreType.DMA
    f32, bf16 = jnp.float32, jnp.bfloat16
    vmem, hbm = pl.BlockSpec(memory_space=pltpu.VMEM), pl.BlockSpec(memory_space=pl.ANY)
    states = pl.pallas_call(
        kernel,
        out_shape=jax.ShapeDtypeStruct((TOK, 2 * HALF), f32),
        in_specs=[hbm, hbm, vmem, vmem, vmem],
        out_specs=hbm,
        scratch_shapes=[
            pltpu.VMEM((ROWS, DEPTH), bf16),
            *[pltpu.VMEM((DEPTH, 3 * w), bf16) for w in WIDTHS],
            pltpu.VMEM((GROUPS, 3, 2, TOK, CH), f32),
            pltpu.VMEM((GROUPS, 2, 2, TOK, CH), f32),
            pltpu.VMEM((GROUPS, 2, 2, TOK, CH), f32),
            pltpu.VMEM((GROUPS, ROWS, CH), f32),
            pltpu.VMEM((2, GROUPS, 2, 3, SEGS, CH), f32),
            pltpu.VMEM((2, GROUPS, SEGS, CH), f32),
            pltpu.VMEM((2, GROUPS, SEGS, CH), f32),
            pltpu.VMEM((2, CHIPS, GROUPS, SEGS, CH), f32),
            dma((CHUNKS + 1,)),
            dma((CHUNKS,)),
            dma((CHUNKS,)),
            dma((CHUNKS,)),
            dma((CHUNKS, 6)),
            dma((CHUNKS, RING, 6)),
            dma((3, 2)),
            dma((3, 2)),
            dma((7,)),
            dma((7,)),
            dma((2, CHUNKS)),
            dma((2, CHUNKS)),
            dma((GROUPS,)),
            dma((GROUPS,)),
            dma((GROUPS,)),
        ],
        compiler_params=pltpu.CompilerParams(
            collective_id=0, has_side_effects=True, vmem_limit_bytes=56 * 2**20
        ),
        cost_estimate=pl.CostEstimate(
            flops=2 * ROWS * DEPTH * 3 * HALF, bytes_accessed=8 * 2**20, transcendentals=0
        ),
    )(tokens, weights, gate_bias, recurrent, initial_state[None, :])
    return pl.pallas_call(
        copy_out,
        out_shape=jax.ShapeDtypeStruct((TOK, 2 * HALF), f32),
        in_specs=[hbm],
        out_specs=hbm,
        scratch_shapes=[pltpu.VMEM((TOK, 2 * HALF), f32), dma((8,)), dma((8,))],
        compiler_params=pltpu.CompilerParams(vmem_limit_bytes=56 * 2**20),
    )(states)


def solution(mesh):
    return jax.shard_map(
        body,
        mesh=mesh,
        in_specs=(P("seq", "tp"), P(None, "seq", "tp"), P(None, "tp"), P(None, "tp"), P("tp")),
        out_specs=P("seq", "tp"),
        check_vma=False,
    )
```

```python
import functools

import jax
import jax.numpy as jnp
from jax import lax
from jax.experimental import pallas as pl
from jax.experimental.pallas import tpu as pltpu
from jax.sharding import PartitionSpec as P

MESH = pl.DeviceIdType.MESH
RING = 4
CHIPS = RING * RING
CH = 128
WIDTHS = (256, 128, 128)
STARTS = (0, 256, 384)
SUBS = ((0, 1), (2,), (3,))
CHUNKS = len(WIDTHS)
HALF = sum(WIDTHS)
GROUPS = HALF // CH
PASSES = ((0, 3), (3, 1))
TOK = 512
ROWS = 2 * TOK
FEAT = 1024
DEPTH = CHIPS * 256
FAR_FIRST = sorted(
    [(i, j) for i in range(RING) for j in range(RING) if i or j],
    key=lambda d: -sum(min(v, RING - v) for v in d),
)
SEGS = 8
SEG = TOK // SEGS


def sigmoid(v):
    return jax.nn.sigmoid(v)


def cell(pre, p, coef):
    u = sigmoid(pre[0] + coef[0] * p)
    r = sigmoid(pre[1] + coef[1] * p)
    c = jnp.tanh(pre[2] + coef[2] * r * p)
    keep = 1.0 - u
    slope = c - p
    jac = (
        keep
        + slope * (u * keep * coef[0])
        + u * ((1.0 - c * c) * coef[2]) * (r + p * (r * (1.0 - r) * coef[1]))
    )
    stepped = keep * p + u * c
    return jac, stepped - jac * p


def cell_at_zero(pre, coef):
    u = sigmoid(pre[0])
    r = sigmoid(pre[1])
    c = jnp.tanh(pre[2])
    keep = 1.0 - u
    jac = keep + c * (u * keep * coef[0]) + u * ((1.0 - c * c) * coef[2]) * r
    return jac, u * c


def kernel(
    tok_hbm, w_hbm, bias, rec, init, out,
    X, W0, W1, W2, PRE, AB1, AB2, OUTB, SEGT, MID, SUM, SLOT,
    local_sem, sib_s, sib_r, w_s, p1_r, p2_r, t_s, t_r, ts_s, ts_r, ex_s, ex_r, o_l, o_s, o_r,
):
    W = (W0, W1, W2)
    ORDER = (0, 3, 1, 2)
    seq, x = lax.axis_index("seq"), lax.axis_index("tp")
    c = lax.rem(seq, 2)
    q = seq // 2
    y, z = q // RING, lax.rem(q, RING)
    p = (1 - c) * y + c * z
    s = (1 - c) * z + c * y

    def block(pp, ss):
        return lax.rem(pp, RING) * (4 - 3 * c) + lax.rem(ss, RING) * (1 + 3 * c)

    def peer(qq):
        return (qq * 2 + c, x)

    right, left = peer(block(p + 1, s)), peer(block(p + 3, s))
    up, down = peer(block(p, s + 1)), peer(block(p, s + 3))
    xr, xl = (seq, lax.rem(x + 1, RING)), (seq, lax.rem(x + 3, RING))
    sib = (q * 2 + 1 - c, x)

    def rcopy(src, dst, ss, rs, dev):
        return pltpu.make_async_remote_copy(
            src_ref=src, dst_ref=dst, send_sem=ss, recv_sem=rs, device_id=dev, device_id_type=MESH
        )

    def send(ref, ss, rs, dev):
        rcopy(ref, ref, ss, rs, dev).start()

    def arrived(ref, sem):
        pltpu.make_async_copy(ref, ref, sem).wait()

    def wrows(k, blk, half=None):
        if half is None:
            return W[k].at[pl.ds(pl.multiple_of(blk * 256, 256), 256)]
        return W[k].at[pl.ds(pl.multiple_of(blk * 256 + half * 128, 128), 128)]

    def chan(core, k):
        return pl.ds(pl.multiple_of(core * HALF + STARTS[k], CH), WIDTHS[k])

    def lanes(core, sub):
        return pl.ds(pl.multiple_of(core * HALF + sub * CH, CH), CH)

    def trows(core, half=None):
        if half is None:
            return pl.ds(pl.multiple_of(core * TOK, TOK), TOK)
        return pl.ds(pl.multiple_of(core * TOK + half * 256, 256), 256)

    def tcols(xx):
        return pl.ds(pl.multiple_of(lax.rem(xx, RING) * FEAT, FEAT), FEAT)

    mine = pl.ds(pl.multiple_of(q * 256 + c * 128, 128), 128)
    own_tok = pltpu.make_async_copy(tok_hbm, X.at[trows(c), tcols(x)], local_sem.at[CHUNKS])
    for k in range(CHUNKS):
        for g in range(3):
            pltpu.make_async_copy(
                w_hbm.at[g, :, chan(c, k)],
                W[k].at[mine, pl.ds(g * WIDTHS[k], WIDTHS[k])],
                local_sem.at[k],
            ).start()
    own_tok.start()

    barrier = pltpu.get_barrier_semaphore()

    for d in (right, left, up, down, xr, xl, sib):
        pl.semaphore_signal(barrier, inc=1, device_id=d, device_id_type=MESH)
    pl.semaphore_wait(barrier, 7)

    def own_rows(k):
        arrived(wrows(k, q, c), local_sem.at[k])
        send(wrows(k, q, c), w_s.at[k], p1_r.at[k, 0], right)
        send(wrows(k, q, c), w_s.at[k], p1_r.at[k, 1], left)

    for k in range(CHUNKS):
        for g in range(3):
            rcopy(
                w_hbm.at[g, :, chan(1 - c, k)],
                W[k].at[mine, pl.ds(g * WIDTHS[k], WIDTHS[k])],
                sib_s.at[k], sib_r.at[k], sib,
            ).start()
        if k == 0:
            own_rows(0)
    own_tok.wait()
    for h in range(2):
        send(X.at[trows(c, h), tcols(x)], t_s.at[0, h], t_r.at[0, h], xr)
        send(X.at[trows(c, 1 - h), tcols(x)], t_s.at[1, 1 - h], t_r.at[1, 1 - h], xl)
    send(X.at[trows(c), tcols(x)], ts_s.at[0], ts_r.at[0], sib)

    def send2(k, i):
        own = block(p + i, s)
        send(wrows(k, own, 0), w_s.at[k], p2_r.at[k, i, 0], up)
        send(wrows(k, own, 1), w_s.at[k], p2_r.at[k, i, 1], down)

    def send2b(k, i):
        own = block(p + i, s)
        send(wrows(k, own, 1), w_s.at[k], p2_r.at[k, i, 4], up)
        send(wrows(k, own, 0), w_s.at[k], p2_r.at[k, i, 5], down)

    def sibling_rows(k):
        arrived(wrows(k, q, 1 - c), sib_r.at[k])
        send(wrows(k, q, 1 - c), w_s.at[k], p1_r.at[k, 2], right)
        send(wrows(k, q, 1 - c), w_s.at[k], p1_r.at[k, 3], left)

    def ring_on(k):
        arrived(wrows(k, block(p + 3, s), c), p1_r.at[k, 0])
        send(wrows(k, block(p + 3, s), c), w_s.at[k], p1_r.at[k, 4], right)
        arrived(wrows(k, block(p + 1, s), c), p1_r.at[k, 1])
        arrived(wrows(k, block(p + 1, s), 1 - c), p1_r.at[k, 3])
        send(wrows(k, block(p + 1, s), 1 - c), w_s.at[k], p1_r.at[k, 5], left)
        arrived(wrows(k, block(p + 3, s), 1 - c), p1_r.at[k, 2])

    def ring_end(k):
        arrived(wrows(k, block(p + 2, s), c), p1_r.at[k, 4])
        arrived(wrows(k, block(p + 2, s), 1 - c), p1_r.at[k, 5])

    def pass_on(k, i):
        below, above = block(p + i, s + 3), block(p + i, s + 1)
        arrived(wrows(k, below, 0), p2_r.at[k, i, 0])
        send(wrows(k, below, 0), w_s.at[k], p2_r.at[k, i, 2], up)
        arrived(wrows(k, above, 1), p2_r.at[k, i, 1])
        send(wrows(k, above, 1), w_s.at[k], p2_r.at[k, i, 3], down)

    def near(k, i):
        arrived(wrows(k, block(p + i, s + 3), 1), p2_r.at[k, i, 4])
        arrived(wrows(k, block(p + i, s + 1), 0), p2_r.at[k, i, 5])

    def far(k, i):
        for h in range(2):
            arrived(wrows(k, block(p + i, s + 2), h), p2_r.at[k, i, 2 + h])

    def gathered(k):
        for i in ORDER:
            near(k, i)
            far(k, i)

    def features_first():
        arrived(X.at[trows(c, 0), tcols(x + 3)], t_r.at[0, 0])
        send(X.at[trows(c, 0), tcols(x + 3)], t_s.at[2, 0], t_r.at[2, 0], xr)
        arrived(X.at[trows(c, 1), tcols(x + 1)], t_r.at[1, 1])
        send(X.at[trows(c, 1), tcols(x + 1)], t_s.at[2, 1], t_r.at[2, 1], xl)
        send(X.at[trows(c, 0), tcols(x + 3)], ts_s.at[1], ts_r.at[1], sib)
        send(X.at[trows(c, 1), tcols(x + 1)], ts_s.at[2], ts_r.at[2], sib)

    def features_second():
        arrived(X.at[trows(c, 1), tcols(x + 3)], t_r.at[0, 1])
        send(X.at[trows(c, 1), tcols(x + 3)], ts_s.at[3], ts_r.at[3], sib)
        arrived(X.at[trows(c, 0), tcols(x + 1)], t_r.at[1, 0])
        send(X.at[trows(c, 0), tcols(x + 1)], ts_s.at[4], ts_r.at[4], sib)

    def features_last():
        for h in range(2):
            arrived(X.at[trows(c, h), tcols(x + 2)], t_r.at[2, h])
            send(X.at[trows(c, h), tcols(x + 2)], ts_s.at[5 + h], ts_r.at[5 + h], sib)

    def sibling_features():
        arrived(X.at[trows(1 - c), tcols(x)], ts_r.at[0])
        for n, (h, d) in enumerate(((0, 3), (1, 1), (1, 3), (0, 1))):
            arrived(X.at[trows(1 - c, h), tcols(x + d)], ts_r.at[1 + n])

    def sibling_last():
        for h in range(2):
            arrived(X.at[trows(1 - c, h), tcols(x + 2)], ts_r.at[5 + h])

    def row_of(ref, g, sub):
        return ref[pl.ds(g, 1), lanes(c, sub)]

    def put(k, acc, t, add):
        m = c if t < 2 else 1 - c
        for n, sub in enumerate(SUBS[k]):
            for g in range(3):
                v = acc[:, g * WIDTHS[k] + n * CH : g * WIDTHS[k] + (n + 1) * CH]
                if not add:
                    v = v + row_of(bias, g, sub)
                for h in range(SEGS // 2):
                    at = pl.ds((t % 2) * (SEGS // 2) + h, SEG, stride=SEGS)
                    part = v[h * SEG : (h + 1) * SEG]
                    PRE[sub, g, m, at, :] = PRE[sub, g, m, at, :] + part if add else part

    def quarter(t):
        return trows(c if t < 2 else 1 - c, t % 2)

    def matmul(k, t, places, add):
        cols = [tcols(x + d) for d in places]
        a = jnp.concatenate([X[quarter(t), d] for d in cols], axis=1)
        b = jnp.concatenate([W[k][d, :] for d in cols], axis=0)
        put(k, jnp.dot(a, b, preferred_element_type=jnp.float32), t, add)

    def matmul_part(k, t, chips, add):
        at = [pl.ds(pl.multiple_of(block(p + i, s + o) * 256, 256), 256) for i, o in chips]
        a = jnp.concatenate([X[quarter(t), d] for d in at], axis=1)
        b = jnp.concatenate([W[k][d, :] for d in at], axis=0)
        put(k, jnp.dot(a, b, preferred_element_type=jnp.float32), t, add)

    def vreg(j):
        return pl.ds(pl.multiple_of(j * SEGS, SEGS), SEGS)

    sublane = lax.broadcasted_iota(jnp.int32, (SEGS, CH), 0)

    def coefs(sub):
        return [jnp.broadcast_to(row_of(rec, g, sub), (SEGS, CH)) for g in range(3)]

    def publish(n, sub, AB):
        tot = []
        for m in range(2):
            SEGT[n, sub, m, 0], SEGT[n, sub, m, 1] = AB[m]
            ta, tb = SEGT[n, sub, m, 0, 0:1], SEGT[n, sub, m, 1, 0:1]
            for i in range(1, SEGS):
                a, b = SEGT[n, sub, m, 0, i : i + 1], SEGT[n, sub, m, 1, i : i + 1]
                ta, tb = a * ta, a * tb + b
            tot.append((ta, tb))
        (a0, b0), (a1, b1) = tot
        MID[n, sub] = jnp.where(sublane == 0, a0, b0)
        SUM[n, sub] = jnp.where(sublane == 0, a0 * a1, a1 * b0 + b1)

    def span(k):
        return pl.ds(*PASSES[k])

    def exchange(n, k):
        for dy, dz in FAR_FIRST:
            there = lax.rem(y + dy, RING) * RING + lax.rem(z + dz, RING)
            rcopy(
                SUM.at[n, span(k)], SLOT.at[n, lax.rem(there - q + CHIPS, CHIPS), span(k)],
                ex_s.at[n, k], ex_r.at[n, k], peer(there),
            ).start()

    def exchanged(n, k, sem):
        arrived(SLOT.at[n, pl.ds(1, CHIPS - 1), span(k)], sem.at[n, k])

    def incoming(n, sub):
        h = row_of(init, 0, sub)
        for e in range(CHIPS - 1, 0, -1):
            h = jnp.where(e <= q, SLOT[n, e, sub, 0:1] * h + SLOT[n, e, sub, 1:2], h)
        starts = [h, MID[n, sub, 0:1] * h + MID[n, sub, 1:2]]
        for m in range(2):
            h = starts[m]
            SEGT[n, sub, m, 2, 0:1] = h
            for i in range(SEGS - 1):
                h = SEGT[n, sub, m, 0, i : i + 1] * h + SEGT[n, sub, m, 1, i : i + 1]
                SEGT[n, sub, m, 2, i + 1 : i + 2] = h
        return [SEGT[n, sub, m, 2] for m in range(2)]

    UN = 16

    def pass1(sub):
        coef = coefs(sub)
        first = (sublane + q) == 0
        p0 = jnp.where(first, jnp.broadcast_to(row_of(init, 0, sub), (SEGS, CH)), 0.0)

        def step(j, AB, p0=None):
            new = []
            for m in range(2):
                v = vreg(j)
                pre = [PRE[sub, g, m, v, :] for g in range(3)]
                a, b = cell_at_zero(pre, coef) if p0 is None or m else cell(pre, p0, coef)
                AB1[sub, 0, m, v, :] = a
                AB1[sub, 1, m, v, :] = b
                new.append((a, b) if AB is None else (a * AB[m][0], a * AB[m][1] + b))
            return new

        AB = step(0, None, p0)
        for j in range(1, UN):
            AB = step(j, AB)

        def group(t, AB):
            for o in range(UN):
                AB = step(t * UN + o, AB)
            return AB

        publish(0, sub, lax.fori_loop(1, SEG // UN, group, AB))

    def pass2(sub):
        coef = coefs(sub)

        def group(t, carry):
            for o in range(UN):
                v = vreg(t * UN + o)
                new = []
                for m in range(2):
                    h, A, B = carry[m]
                    a, b = cell([PRE[sub, g, m, v, :] for g in range(3)], h, coef)
                    AB2[sub, 0, m, v, :] = a
                    AB2[sub, 1, m, v, :] = b
                    h = AB1[sub, 0, m, v, :] * h + AB1[sub, 1, m, v, :]
                    new.append((h, a * A, a * B + b))
                carry = new
            return carry

        one, zero = jnp.ones((SEGS, CH), jnp.float32), jnp.zeros((SEGS, CH), jnp.float32)
        carry = lax.fori_loop(0, SEG // UN, group, [(h, one, zero) for h in incoming(0, sub)])
        publish(1, sub, [(A, B) for _, A, B in carry])

    def pass3(sub):
        def group(t, hs):
            for o in range(UN):
                j = t * UN + o
                v = vreg(j)
                hs = [AB2[sub, 0, m, v, :] * hs[m] + AB2[sub, 1, m, v, :] for m in range(2)]
                for m in range(2):
                    OUTB[sub, pl.ds(m * TOK + j, SEGS, stride=SEG), :] = hs[m]
            return hs

        lax.fori_loop(0, SEG // UN, group, incoming(1, sub))
        here = out.at[:, lanes(c, sub)]
        rcopy(OUTB.at[sub, trows(1 - c)], here, o_s.at[sub], o_r.at[sub], sib).start()
        pltpu.make_async_copy(OUTB.at[sub, trows(c)], here, o_l.at[sub]).start()

    def put_out(sub):
        here, there = out.at[:, lanes(c, sub)], out.at[:, lanes(1 - c, sub)]
        arrived(here, o_l.at[sub])
        arrived(here, o_s.at[sub])
        arrived(there, o_r.at[sub])

    def first_pass(k):
        for sub in SUBS[k]:
            pass1(sub)
        if k > 0:
            exchange(0, k - 1)

    def second_pass(k):
        exchanged(0, k, ex_r)
        for sub in range(PASSES[k][0], sum(PASSES[k])):
            pass2(sub)
        exchange(1, k)

    def last_pass(k):
        exchanged(1, k, ex_r)
        for sub in range(PASSES[k][0], sum(PASSES[k])):
            pass3(sub)

    def sent(k):
        arrived(wrows(k, q, c), sib_s.at[k])
        arrived(W[k].at[pl.ds(0, 30 * 128)], w_s.at[k])

    def sent_features():
        for h in range(2):
            for d in range(3):
                arrived(X.at[trows(c, h), tcols(x)], t_s.at[d, h])
        arrived(X.at[trows(c), tcols(x)], ts_s.at[0])
        for n in range(6):
            arrived(X.at[trows(c, 0), tcols(x)], ts_s.at[1 + n])

    sibling_rows(0)
    send2(0, 0)
    send2b(0, 0)
    ring_on(0)
    for i in (3, 1):
        send2(0, i)
        send2b(0, i)
    ring_end(0)
    send2(0, 2)
    send2b(0, 2)
    features_first()
    pass_on(0, 0)
    pass_on(0, 3)
    own_rows(1)
    sibling_rows(1)
    pass_on(0, 1)
    pass_on(0, 2)
    features_second()
    ring_on(1)
    ring_end(1)
    for i in ORDER:
        send2(1, i)
        send2b(1, i)
    own_rows(2)
    sibling_rows(2)
    gathered(0)
    matmul(0, 0, (0, 3, 1), False)
    ring_on(2)
    matmul(0, 1, (0, 3, 1), False)
    ring_end(2)
    send2(2, 0)
    send2b(2, 0)
    pass_on(1, 0)
    sibling_features()
    matmul(0, 2, (0, 3, 1), False)
    features_last()
    pass_on(1, 3)
    matmul(0, 3, (0, 3, 1), False)
    pass_on(1, 1)
    send2(2, 3)
    send2b(2, 3)
    matmul(0, 0, (2,), True)
    matmul(0, 1, (2,), True)
    pass_on(1, 2)
    sibling_last()
    matmul(0, 2, (2,), True)
    matmul(0, 3, (2,), True)
    first_pass(0)
    for i in (1, 2):
        send2(2, i)
        send2b(2, i)
    for i in ORDER:
        near(1, i)
    for t in range(4):
        matmul_part(1, t, [(i, o) for o in (0, 1, 3) for i in ORDER], False)
        if t % 2 == 1:
            pass_on(2, ORDER[t // 2])
    for i in ORDER:
        far(1, i)
    for t in range(4):
        matmul_part(1, t, [(i, 2) for i in ORDER], True)
    first_pass(1)
    pass_on(2, 1)
    pass_on(2, 2)
    for i in ORDER:
        near(2, i)
    for t in range(4):
        matmul_part(2, t, [(i, o) for o in (0, 1, 3) for i in ORDER], False)
    far(2, 0)
    far(2, 3)
    for t in range(4):
        matmul_part(2, t, [(i, 2) for i in (0, 3)], True)
    far(2, 1)
    far(2, 2)
    for t in range(4):
        matmul_part(2, t, [(i, 2) for i in (1, 2)], True)
    first_pass(2)
    second_pass(0)
    second_pass(1)
    for k in range(CHUNKS):
        sent(k)
    sent_features()
    exchanged(0, 0, ex_s)
    exchanged(0, 1, ex_s)
    last_pass(0)
    exchanged(1, 0, ex_s)
    last_pass(1)
    exchanged(1, 1, ex_s)
    for sub in range(GROUPS):
        put_out(sub)


def copy_out(src, dst, buf, load, store):
    rows = TOK // 8
    ins = [
        pltpu.make_async_copy(src.at[pl.ds(i * rows, rows)], buf.at[pl.ds(i * rows, rows)], load.at[i])
        for i in range(8)
    ]
    outs = [
        pltpu.make_async_copy(buf.at[pl.ds(i * rows, rows)], dst.at[pl.ds(i * rows, rows)], store.at[i])
        for i in range(8)
    ]
    for cp in ins:
        cp.start()
    for cp, nxt in zip(ins, outs):
        cp.wait()
        nxt.start()
    for cp in outs:
        cp.wait()


def body(tokens, weights, gate_bias, recurrent, initial_state):
    dma = pltpu.SemaphoreType.DMA
    f32, bf16 = jnp.float32, jnp.bfloat16
    vmem, hbm = pl.BlockSpec(memory_space=pltpu.VMEM), pl.BlockSpec(memory_space=pl.ANY)
    states = pl.pallas_call(
        kernel,
        out_shape=jax.ShapeDtypeStruct((TOK, 2 * HALF), f32),
        in_specs=[hbm, hbm, vmem, vmem, vmem],
        out_specs=hbm,
        scratch_shapes=[
            pltpu.VMEM((ROWS, DEPTH), bf16),
            *[pltpu.VMEM((DEPTH, 3 * w), bf16) for w in WIDTHS],
            pltpu.VMEM((GROUPS, 3, 2, TOK, CH), f32),
            pltpu.VMEM((GROUPS, 2, 2, TOK, CH), f32),
            pltpu.VMEM((GROUPS, 2, 2, TOK, CH), f32),
            pltpu.VMEM((GROUPS, ROWS, CH), f32),
            pltpu.VMEM((2, GROUPS, 2, 3, SEGS, CH), f32),
            pltpu.VMEM((2, GROUPS, SEGS, CH), f32),
            pltpu.VMEM((2, GROUPS, SEGS, CH), f32),
            pltpu.VMEM((2, CHIPS, GROUPS, SEGS, CH), f32),
            dma((CHUNKS + 1,)),
            dma((CHUNKS,)),
            dma((CHUNKS,)),
            dma((CHUNKS,)),
            dma((CHUNKS, 6)),
            dma((CHUNKS, RING, 6)),
            dma((3, 2)),
            dma((3, 2)),
            dma((7,)),
            dma((7,)),
            dma((2, len(PASSES))),
            dma((2, len(PASSES))),
            dma((GROUPS,)),
            dma((GROUPS,)),
            dma((GROUPS,)),
        ],
        compiler_params=pltpu.CompilerParams(
            collective_id=0, has_side_effects=True, vmem_limit_bytes=56 * 2**20
        ),
        cost_estimate=pl.CostEstimate(
            flops=2 * ROWS * DEPTH * 3 * HALF, bytes_accessed=8 * 2**20, transcendentals=0
        ),
    )(tokens, weights, gate_bias, recurrent, initial_state[None, :])
    return pl.pallas_call(
        copy_out,
        out_shape=jax.ShapeDtypeStruct((TOK, 2 * HALF), f32),
        in_specs=[hbm],
        out_specs=hbm,
        scratch_shapes=[pltpu.VMEM((TOK, 2 * HALF), f32), dma((8,)), dma((8,))],
        compiler_params=pltpu.CompilerParams(vmem_limit_bytes=56 * 2**20),
    )(states)


def solution(mesh):
    return jax.shard_map(
        body,
        mesh=mesh,
        in_specs=(P("seq", "tp"), P(None, "seq", "tp"), P(None, "tp"), P(None, "tp"), P("tp")),
        out_specs=P("seq", "tp"),
        check_vma=False,
    )
```

```python
import functools

import jax
import jax.numpy as jnp
from jax import lax
from jax.experimental import pallas as pl
from jax.experimental.pallas import tpu as pltpu
from jax.sharding import PartitionSpec as P

MESH = pl.DeviceIdType.MESH
RING = 4
CHIPS = RING * RING
CH = 128
WIDTHS = (256, 128, 128)
STARTS = (0, 256, 384)
SUBS = ((0, 1), (2,), (3,))
CHUNKS = len(WIDTHS)
HALF = sum(WIDTHS)
GROUPS = HALF // CH
PASSES = ((0, 3), (3, 1))
TOK = 512
ROWS = 2 * TOK
FEAT = 1024
DEPTH = CHIPS * 256
FAR_FIRST = sorted(
    [(i, j) for i in range(RING) for j in range(RING) if i or j],
    key=lambda d: -sum(min(v, RING - v) for v in d),
)
SEGS = 8
SEG = TOK // SEGS


def sigmoid(v):
    return jax.nn.sigmoid(v)


def cell(pre, p, coef):
    u = sigmoid(pre[0] + coef[0] * p)
    r = sigmoid(pre[1] + coef[1] * p)
    c = jnp.tanh(pre[2] + coef[2] * r * p)
    keep = 1.0 - u
    slope = c - p
    jac = (
        keep
        + slope * (u * keep * coef[0])
        + u * ((1.0 - c * c) * coef[2]) * (r + p * (r * (1.0 - r) * coef[1]))
    )
    stepped = keep * p + u * c
    return jac, stepped - jac * p


def cell_at_zero(pre, coef):
    u = sigmoid(pre[0])
    r = sigmoid(pre[1])
    c = jnp.tanh(pre[2])
    keep = 1.0 - u
    jac = keep + c * (u * keep * coef[0]) + u * ((1.0 - c * c) * coef[2]) * r
    return jac, u * c


def kernel(
    tok_hbm, w_hbm, bias_hbm, rec_hbm, init_hbm, out,
    X, W0, W1, W2, bias, rec, init, PRE, AB1, AB2, OUTB, SEGT, MID, SUM, SLOT,
    local_sem, sib_s, sib_r, w_s, p1_r, p2_r, t_s, t_r, ts_s, ts_r, ex_s, ex_r, o_l, o_s, o_r,
):
    W = (W0, W1, W2)
    ORDER = (0, 3, 1, 2)
    seq, x = lax.axis_index("seq"), lax.axis_index("tp")
    c = lax.rem(seq, 2)
    q = seq // 2
    y, z = q // RING, lax.rem(q, RING)
    p = (1 - c) * y + c * z
    s = (1 - c) * z + c * y

    def block(pp, ss):
        return lax.rem(pp, RING) * (4 - 3 * c) + lax.rem(ss, RING) * (1 + 3 * c)

    def peer(qq):
        return (qq * 2 + c, x)

    right, left = peer(block(p + 1, s)), peer(block(p + 3, s))
    up, down = peer(block(p, s + 1)), peer(block(p, s + 3))
    xr, xl = (seq, lax.rem(x + 1, RING)), (seq, lax.rem(x + 3, RING))
    sib = (q * 2 + 1 - c, x)

    def rcopy(src, dst, ss, rs, dev):
        return pltpu.make_async_remote_copy(
            src_ref=src, dst_ref=dst, send_sem=ss, recv_sem=rs, device_id=dev, device_id_type=MESH
        )

    def send(ref, ss, rs, dev):
        rcopy(ref, ref, ss, rs, dev).start()

    def arrived(ref, sem):
        pltpu.make_async_copy(ref, ref, sem).wait()

    def wrows(k, blk, half=None):
        if half is None:
            return W[k].at[pl.ds(pl.multiple_of(blk * 256, 256), 256)]
        return W[k].at[pl.ds(pl.multiple_of(blk * 256 + half * 128, 128), 128)]

    def chan(core, k):
        return pl.ds(pl.multiple_of(core * HALF + STARTS[k], CH), WIDTHS[k])

    def lanes(core, sub):
        return pl.ds(pl.multiple_of(core * HALF + sub * CH, CH), CH)

    def trows(core, half=None):
        if half is None:
            return pl.ds(pl.multiple_of(core * TOK, TOK), TOK)
        return pl.ds(pl.multiple_of(core * TOK + half * 256, 256), 256)

    def tcols(xx):
        return pl.ds(pl.multiple_of(lax.rem(xx, RING) * FEAT, FEAT), FEAT)

    barrier = pltpu.get_barrier_semaphore()

    for d in (right, left, up, down, xr, xl, sib):
        pl.semaphore_signal(barrier, inc=1, device_id=d, device_id_type=MESH)
    mine = pl.ds(pl.multiple_of(q * 256 + c * 128, 128), 128)
    own_tok = pltpu.make_async_copy(tok_hbm, X.at[trows(c), tcols(x)], local_sem.at[CHUNKS])
    for k in range(CHUNKS):
        for g in range(3):
            pltpu.make_async_copy(
                w_hbm.at[g, :, chan(c, k)],
                W[k].at[mine, pl.ds(g * WIDTHS[k], WIDTHS[k])],
                local_sem.at[k],
            ).start()
    own_tok.start()
    small = [
        pltpu.make_async_copy(src, dst, local_sem.at[CHUNKS + 1 + n])
        for n, (src, dst) in enumerate(((bias_hbm, bias), (rec_hbm, rec), (init_hbm, init)))
    ]
    for cp in small:
        cp.start()

    pl.semaphore_wait(barrier, 7)

    def own_rows(k):
        arrived(wrows(k, q, c), local_sem.at[k])
        send(wrows(k, q, c), w_s.at[k], p1_r.at[k, 0], right)
        send(wrows(k, q, c), w_s.at[k], p1_r.at[k, 1], left)

    for k in range(CHUNKS):
        for g in range(3):
            rcopy(
                w_hbm.at[g, :, chan(1 - c, k)],
                W[k].at[mine, pl.ds(g * WIDTHS[k], WIDTHS[k])],
                sib_s.at[k], sib_r.at[k], sib,
            ).start()
        if k == 0:
            own_rows(0)
    own_tok.wait()
    for h in range(2):
        send(X.at[trows(c, h), tcols(x)], t_s.at[0, h], t_r.at[0, h], xr)
        send(X.at[trows(c, 1 - h), tcols(x)], t_s.at[1, 1 - h], t_r.at[1, 1 - h], xl)
    send(X.at[trows(c), tcols(x)], ts_s.at[0], ts_r.at[0], sib)

    def send2(k, i):
        own = block(p + i, s)
        send(wrows(k, own, 0), w_s.at[k], p2_r.at[k, i, 0], up)
        send(wrows(k, own, 1), w_s.at[k], p2_r.at[k, i, 1], down)

    def send2b(k, i):
        own = block(p + i, s)
        send(wrows(k, own, 1), w_s.at[k], p2_r.at[k, i, 4], up)
        send(wrows(k, own, 0), w_s.at[k], p2_r.at[k, i, 5], down)

    def sibling_rows(k):
        arrived(wrows(k, q, 1 - c), sib_r.at[k])
        send(wrows(k, q, 1 - c), w_s.at[k], p1_r.at[k, 2], right)
        send(wrows(k, q, 1 - c), w_s.at[k], p1_r.at[k, 3], left)

    def ring_on(k):
        arrived(wrows(k, block(p + 3, s), c), p1_r.at[k, 0])
        send(wrows(k, block(p + 3, s), c), w_s.at[k], p1_r.at[k, 4], right)
        arrived(wrows(k, block(p + 1, s), c), p1_r.at[k, 1])
        arrived(wrows(k, block(p + 1, s), 1 - c), p1_r.at[k, 3])
        send(wrows(k, block(p + 1, s), 1 - c), w_s.at[k], p1_r.at[k, 5], left)
        arrived(wrows(k, block(p + 3, s), 1 - c), p1_r.at[k, 2])

    def ring_end(k):
        arrived(wrows(k, block(p + 2, s), c), p1_r.at[k, 4])
        arrived(wrows(k, block(p + 2, s), 1 - c), p1_r.at[k, 5])

    def pass_on(k, i):
        below, above = block(p + i, s + 3), block(p + i, s + 1)
        arrived(wrows(k, below, 0), p2_r.at[k, i, 0])
        send(wrows(k, below, 0), w_s.at[k], p2_r.at[k, i, 2], up)
        arrived(wrows(k, above, 1), p2_r.at[k, i, 1])
        send(wrows(k, above, 1), w_s.at[k], p2_r.at[k, i, 3], down)

    def near(k, i):
        arrived(wrows(k, block(p + i, s + 3), 1), p2_r.at[k, i, 4])
        arrived(wrows(k, block(p + i, s + 1), 0), p2_r.at[k, i, 5])

    def far(k, i):
        for h in range(2):
            arrived(wrows(k, block(p + i, s + 2), h), p2_r.at[k, i, 2 + h])

    def gathered(k):
        for i in ORDER:
            near(k, i)
            far(k, i)

    def features_first():
        arrived(X.at[trows(c, 0), tcols(x + 3)], t_r.at[0, 0])
        send(X.at[trows(c, 0), tcols(x + 3)], t_s.at[2, 0], t_r.at[2, 0], xr)
        arrived(X.at[trows(c, 1), tcols(x + 1)], t_r.at[1, 1])
        send(X.at[trows(c, 1), tcols(x + 1)], t_s.at[2, 1], t_r.at[2, 1], xl)
        send(X.at[trows(c, 0), tcols(x + 3)], ts_s.at[1], ts_r.at[1], sib)
        send(X.at[trows(c, 1), tcols(x + 1)], ts_s.at[2], ts_r.at[2], sib)

    def features_second():
        arrived(X.at[trows(c, 1), tcols(x + 3)], t_r.at[0, 1])
        send(X.at[trows(c, 1), tcols(x + 3)], ts_s.at[3], ts_r.at[3], sib)
        arrived(X.at[trows(c, 0), tcols(x + 1)], t_r.at[1, 0])
        send(X.at[trows(c, 0), tcols(x + 1)], ts_s.at[4], ts_r.at[4], sib)

    def features_last():
        for h in range(2):
            arrived(X.at[trows(c, h), tcols(x + 2)], t_r.at[2, h])
            send(X.at[trows(c, h), tcols(x + 2)], ts_s.at[5 + h], ts_r.at[5 + h], sib)

    def sibling_features():
        arrived(X.at[trows(1 - c), tcols(x)], ts_r.at[0])
        for n, (h, d) in enumerate(((0, 3), (1, 1), (1, 3), (0, 1))):
            arrived(X.at[trows(1 - c, h), tcols(x + d)], ts_r.at[1 + n])

    def sibling_last():
        for h in range(2):
            arrived(X.at[trows(1 - c, h), tcols(x + 2)], ts_r.at[5 + h])

    def row_of(ref, g, sub):
        return ref[pl.ds(g, 1), lanes(c, sub)]

    def put(k, acc, t, add):
        m = c if t < 2 else 1 - c
        for n, sub in enumerate(SUBS[k]):
            for g in range(3):
                v = acc[:, g * WIDTHS[k] + n * CH : g * WIDTHS[k] + (n + 1) * CH]
                if not add:
                    v = v + row_of(bias, g, sub)
                for h in range(SEGS // 2):
                    at = pl.ds((t % 2) * (SEGS // 2) + h, SEG, stride=SEGS)
                    part = v[h * SEG : (h + 1) * SEG]
                    PRE[sub, g, m, at, :] = PRE[sub, g, m, at, :] + part if add else part

    def quarter(t):
        return trows(c if t < 2 else 1 - c, t % 2)

    def matmul(k, t, places, add):
        cols = [tcols(x + d) for d in places]
        a = jnp.concatenate([X[quarter(t), d] for d in cols], axis=1)
        b = jnp.concatenate([W[k][d, :] for d in cols], axis=0)
        put(k, jnp.dot(a, b, preferred_element_type=jnp.float32), t, add)

    def matmul_part(k, t, chips, add):
        at = [pl.ds(pl.multiple_of(block(p + i, s + o) * 256, 256), 256) for i, o in chips]
        a = jnp.concatenate([X[quarter(t), d] for d in at], axis=1)
        b = jnp.concatenate([W[k][d, :] for d in at], axis=0)
        put(k, jnp.dot(a, b, preferred_element_type=jnp.float32), t, add)

    def vreg(j):
        return pl.ds(pl.multiple_of(j * SEGS, SEGS), SEGS)

    sublane = lax.broadcasted_iota(jnp.int32, (SEGS, CH), 0)

    def coefs(sub):
        return [jnp.broadcast_to(row_of(rec, g, sub), (SEGS, CH)) for g in range(3)]

    def publish(n, sub, AB):
        tot = []
        for m in range(2):
            SEGT[n, sub, m, 0], SEGT[n, sub, m, 1] = AB[m]
            ta, tb = SEGT[n, sub, m, 0, 0:1], SEGT[n, sub, m, 1, 0:1]
            for i in range(1, SEGS):
                a, b = SEGT[n, sub, m, 0, i : i + 1], SEGT[n, sub, m, 1, i : i + 1]
                ta, tb = a * ta, a * tb + b
            tot.append((ta, tb))
        (a0, b0), (a1, b1) = tot
        MID[n, sub] = jnp.where(sublane == 0, a0, b0)
        SUM[n, sub] = jnp.where(sublane == 0, a0 * a1, a1 * b0 + b1)

    def span(k):
        return pl.ds(*PASSES[k])

    def exchange(n, k):
        for dy, dz in FAR_FIRST:
            there = lax.rem(y + dy, RING) * RING + lax.rem(z + dz, RING)
            rcopy(
                SUM.at[n, span(k)], SLOT.at[n, lax.rem(there - q + CHIPS, CHIPS), span(k)],
                ex_s.at[n, k], ex_r.at[n, k], peer(there),
            ).start()

    def exchanged(n, k, sem):
        arrived(SLOT.at[n, pl.ds(1, CHIPS - 1), span(k)], sem.at[n, k])

    def incoming(n, sub):
        h = row_of(init, 0, sub)
        for e in range(CHIPS - 1, 0, -1):
            h = jnp.where(e <= q, SLOT[n, e, sub, 0:1] * h + SLOT[n, e, sub, 1:2], h)
        starts = [h, MID[n, sub, 0:1] * h + MID[n, sub, 1:2]]
        for m in range(2):
            h = starts[m]
            SEGT[n, sub, m, 2, 0:1] = h
            for i in range(SEGS - 1):
                h = SEGT[n, sub, m, 0, i : i + 1] * h + SEGT[n, sub, m, 1, i : i + 1]
                SEGT[n, sub, m, 2, i + 1 : i + 2] = h
        return [SEGT[n, sub, m, 2] for m in range(2)]

    UN = 16

    def pass1(sub):
        coef = coefs(sub)
        first = (sublane + q) == 0
        p0 = jnp.where(first, jnp.broadcast_to(row_of(init, 0, sub), (SEGS, CH)), 0.0)

        def step(j, AB, p0=None):
            new = []
            for m in range(2):
                v = vreg(j)
                pre = [PRE[sub, g, m, v, :] for g in range(3)]
                a, b = cell_at_zero(pre, coef) if p0 is None or m else cell(pre, p0, coef)
                AB1[sub, 0, m, v, :] = a
                AB1[sub, 1, m, v, :] = b
                new.append((a, b) if AB is None else (a * AB[m][0], a * AB[m][1] + b))
            return new

        AB = step(0, None, p0)
        for j in range(1, UN):
            AB = step(j, AB)

        def group(t, AB):
            for o in range(UN):
                AB = step(t * UN + o, AB)
            return AB

        publish(0, sub, lax.fori_loop(1, SEG // UN, group, AB))

    def pass2(sub):
        coef = coefs(sub)

        def group(t, carry):
            for o in range(UN):
                v = vreg(t * UN + o)
                new = []
                for m in range(2):
                    h, A, B = carry[m]
                    a, b = cell([PRE[sub, g, m, v, :] for g in range(3)], h, coef)
                    AB2[sub, 0, m, v, :] = a
                    AB2[sub, 1, m, v, :] = b
                    h = AB1[sub, 0, m, v, :] * h + AB1[sub, 1, m, v, :]
                    new.append((h, a * A, a * B + b))
                carry = new
            return carry

        one, zero = jnp.ones((SEGS, CH), jnp.float32), jnp.zeros((SEGS, CH), jnp.float32)
        carry = lax.fori_loop(0, SEG // UN, group, [(h, one, zero) for h in incoming(0, sub)])
        publish(1, sub, [(A, B) for _, A, B in carry])

    def pass3(sub):
        def group(t, hs):
            for o in range(UN):
                j = t * UN + o
                v = vreg(j)
                hs = [AB2[sub, 0, m, v, :] * hs[m] + AB2[sub, 1, m, v, :] for m in range(2)]
                for m in range(2):
                    OUTB[sub, pl.ds(m * TOK + j, SEGS, stride=SEG), :] = hs[m]
            return hs

        lax.fori_loop(0, SEG // UN, group, incoming(1, sub))
        here = out.at[:, lanes(c, sub)]
        rcopy(OUTB.at[sub, trows(1 - c)], here, o_s.at[sub], o_r.at[sub], sib).start()
        pltpu.make_async_copy(OUTB.at[sub, trows(c)], here, o_l.at[sub]).start()

    def put_out(sub):
        here, there = out.at[:, lanes(c, sub)], out.at[:, lanes(1 - c, sub)]
        arrived(here, o_l.at[sub])
        arrived(here, o_s.at[sub])
        arrived(there, o_r.at[sub])

    def first_pass(k):
        for sub in SUBS[k]:
            pass1(sub)
        if k > 0:
            exchange(0, k - 1)

    def second_pass(k):
        exchanged(0, k, ex_r)
        for sub in range(PASSES[k][0], sum(PASSES[k])):
            pass2(sub)
        exchange(1, k)

    def last_pass(k):
        exchanged(1, k, ex_r)
        for sub in range(PASSES[k][0], sum(PASSES[k])):
            pass3(sub)

    def sent(k):
        arrived(wrows(k, q, c), sib_s.at[k])
        arrived(W[k].at[pl.ds(0, 30 * 128)], w_s.at[k])

    def sent_features():
        for h in range(2):
            for d in range(3):
                arrived(X.at[trows(c, h), tcols(x)], t_s.at[d, h])
        arrived(X.at[trows(c), tcols(x)], ts_s.at[0])
        for n in range(6):
            arrived(X.at[trows(c, 0), tcols(x)], ts_s.at[1 + n])

    sibling_rows(0)
    send2(0, 0)
    send2b(0, 0)
    ring_on(0)
    for i in (3, 1):
        send2(0, i)
        send2b(0, i)
    ring_end(0)
    send2(0, 2)
    send2b(0, 2)
    features_first()
    for cp in small:
        cp.wait()
    pass_on(0, 0)
    pass_on(0, 3)
    own_rows(1)
    sibling_rows(1)
    pass_on(0, 1)
    pass_on(0, 2)
    features_second()
    ring_on(1)
    ring_end(1)
    for i in ORDER:
        send2(1, i)
        send2b(1, i)
    own_rows(2)
    sibling_rows(2)
    gathered(0)
    matmul(0, 0, (0, 3, 1), False)
    ring_on(2)
    matmul(0, 1, (0, 3, 1), False)
    ring_end(2)
    send2(2, 0)
    send2b(2, 0)
    pass_on(1, 0)
    sibling_features()
    matmul(0, 2, (0, 3, 1), False)
    features_last()
    pass_on(1, 3)
    matmul(0, 3, (0, 3, 1), False)
    pass_on(1, 1)
    send2(2, 3)
    send2b(2, 3)
    matmul(0, 0, (2,), True)
    matmul(0, 1, (2,), True)
    pass_on(1, 2)
    sibling_last()
    matmul(0, 2, (2,), True)
    matmul(0, 3, (2,), True)
    first_pass(0)
    for i in (1, 2):
        send2(2, i)
        send2b(2, i)
    for i in ORDER:
        near(1, i)
    for t in range(4):
        matmul_part(1, t, [(i, o) for o in (0, 1, 3) for i in ORDER], False)
        if t % 2 == 1:
            pass_on(2, ORDER[t // 2])
    for i in ORDER:
        far(1, i)
    for t in range(4):
        matmul_part(1, t, [(i, 2) for i in ORDER], True)
    first_pass(1)
    pass_on(2, 1)
    pass_on(2, 2)
    for i in ORDER:
        near(2, i)
    for t in range(4):
        matmul_part(2, t, [(i, o) for o in (0, 1, 3) for i in ORDER], False)
    far(2, 0)
    far(2, 3)
    for t in range(4):
        matmul_part(2, t, [(i, 2) for i in (0, 3)], True)
    far(2, 1)
    far(2, 2)
    for t in range(4):
        matmul_part(2, t, [(i, 2) for i in (1, 2)], True)
    first_pass(2)
    second_pass(0)
    second_pass(1)
    for k in range(CHUNKS):
        sent(k)
    sent_features()
    exchanged(0, 0, ex_s)
    exchanged(0, 1, ex_s)
    last_pass(0)
    exchanged(1, 0, ex_s)
    last_pass(1)
    exchanged(1, 1, ex_s)
    for sub in range(GROUPS):
        put_out(sub)


def copy_out(src, dst, store):
    rows = TOK // 8
    outs = [
        pltpu.make_async_copy(src.at[pl.ds(i * rows, rows)], dst.at[pl.ds(i * rows, rows)], store.at[i])
        for i in range(8)
    ]
    for cp in outs:
        cp.start()
    for cp in outs:
        cp.wait()


def body(tokens, weights, gate_bias, recurrent, initial_state):
    dma = pltpu.SemaphoreType.DMA
    f32, bf16 = jnp.float32, jnp.bfloat16
    hbm = pl.BlockSpec(memory_space=pl.ANY)
    args = (tokens, weights, gate_bias, recurrent, initial_state[None, :])
    args = [pltpu.with_memory_space_constraint(a, pltpu.HBM) for a in args]
    states = pl.pallas_call(
        kernel,
        out_shape=jax.ShapeDtypeStruct((TOK, 2 * HALF), f32),
        in_specs=[hbm] * 5,
        out_specs=hbm,
        scratch_shapes=[
            pltpu.VMEM((ROWS, DEPTH), bf16),
            *[pltpu.VMEM((DEPTH, 3 * w), bf16) for w in WIDTHS],
            pltpu.VMEM((3, 2 * HALF), f32),
            pltpu.VMEM((3, 2 * HALF), f32),
            pltpu.VMEM((1, 2 * HALF), f32),
            pltpu.VMEM((GROUPS, 3, 2, TOK, CH), f32),
            pltpu.VMEM((GROUPS, 2, 2, TOK, CH), f32),
            pltpu.VMEM((GROUPS, 2, 2, TOK, CH), f32),
            pltpu.VMEM((GROUPS, ROWS, CH), f32),
            pltpu.VMEM((2, GROUPS, 2, 3, SEGS, CH), f32),
            pltpu.VMEM((2, GROUPS, SEGS, CH), f32),
            pltpu.VMEM((2, GROUPS, SEGS, CH), f32),
            pltpu.VMEM((2, CHIPS, GROUPS, SEGS, CH), f32),
            dma((CHUNKS + 4,)),
            dma((CHUNKS,)),
            dma((CHUNKS,)),
            dma((CHUNKS,)),
            dma((CHUNKS, 6)),
            dma((CHUNKS, RING, 6)),
            dma((3, 2)),
            dma((3, 2)),
            dma((7,)),
            dma((7,)),
            dma((2, len(PASSES))),
            dma((2, len(PASSES))),
            dma((GROUPS,)),
            dma((GROUPS,)),
            dma((GROUPS,)),
        ],
        compiler_params=pltpu.CompilerParams(
            collective_id=0, has_side_effects=True, vmem_limit_bytes=47 * 2**20
        ),
        cost_estimate=pl.CostEstimate(
            flops=2 * ROWS * DEPTH * 3 * HALF, bytes_accessed=8 * 2**20, transcendentals=0
        ),
    )(*args)
    return pl.pallas_call(
        copy_out,
        out_shape=jax.ShapeDtypeStruct((TOK, 2 * HALF), f32),
        in_specs=[pl.BlockSpec(memory_space=pltpu.VMEM)],
        out_specs=hbm,
        scratch_shapes=[dma((8,))],
        compiler_params=pltpu.CompilerParams(vmem_limit_bytes=16 * 2**20),
    )(states)


def solution(mesh):
    return jax.shard_map(
        body,
        mesh=mesh,
        in_specs=(P("seq", "tp"), P(None, "seq", "tp"), P(None, "tp"), P(None, "tp"), P("tp")),
        out_specs=P("seq", "tp"),
        check_vma=False,
    )
```

```python
import functools

import jax
import jax.numpy as jnp
from jax import lax
from jax.experimental import pallas as pl
from jax.experimental.pallas import tpu as pltpu
from jax.sharding import PartitionSpec as P

MESH = pl.DeviceIdType.MESH
RING = 4
CHIPS = RING * RING
CH = 128
WIDTHS = (256, 128, 128)
STARTS = (0, 256, 384)
SUBS = ((0, 1), (2,), (3,))
CHUNKS = len(WIDTHS)
HALF = sum(WIDTHS)
GROUPS = HALF // CH
PASSES = ((0, 3), (3, 1))
TOK = 512
ROWS = 2 * TOK
FEAT = 1024
DEPTH = CHIPS * 256
FAR_FIRST = sorted(
    [(i, j) for i in range(RING) for j in range(RING) if i or j],
    key=lambda d: -sum(min(v, RING - v) for v in d),
)
SEGS = 8
SEG = TOK // SEGS


def sigmoid(v):
    return jax.nn.sigmoid(v)


def cell(pre, p, coef):
    u = sigmoid(pre[0] + coef[0] * p)
    r = sigmoid(pre[1] + coef[1] * p)
    c = jnp.tanh(pre[2] + coef[2] * r * p)
    keep = 1.0 - u
    slope = c - p
    jac = (
        keep
        + slope * (u * keep * coef[0])
        + u * ((1.0 - c * c) * coef[2]) * (r + p * (r * (1.0 - r) * coef[1]))
    )
    stepped = keep * p + u * c
    return jac, stepped - jac * p


def cell_at_zero(pre, coef):
    u = sigmoid(pre[0])
    r = sigmoid(pre[1])
    c = jnp.tanh(pre[2])
    keep = 1.0 - u
    jac = keep + c * (u * keep * coef[0]) + u * ((1.0 - c * c) * coef[2]) * r
    return jac, u * c


def kernel(
    tok_hbm, w_hbm, bias_hbm, rec_hbm, init_hbm, out,
    X, W0, W1, W2, bias, rec, init, PRE, AB1, AB2, OUTB, SEGT, MID, SUM, SLOT,
    local_sem, sib_s, sib_r, w_s, p1_r, p2_r, t_s, t_r, ts_s, ts_r, ex_s, ex_r, o_l, o_s, o_r,
):
    W = (W0, W1, W2)
    ORDER = (0, 3, 1, 2)
    seq, x = lax.axis_index("seq"), lax.axis_index("tp")
    c = lax.rem(seq, 2)
    q = seq // 2
    y, z = q // RING, lax.rem(q, RING)
    p = (1 - c) * y + c * z
    s = (1 - c) * z + c * y

    def block(pp, ss):
        return lax.rem(pp, RING) * (4 - 3 * c) + lax.rem(ss, RING) * (1 + 3 * c)

    def peer(qq):
        return (qq * 2 + c, x)

    right, left = peer(block(p + 1, s)), peer(block(p + 3, s))
    up, down = peer(block(p, s + 1)), peer(block(p, s + 3))
    xr, xl = (seq, lax.rem(x + 1, RING)), (seq, lax.rem(x + 3, RING))
    sib = (q * 2 + 1 - c, x)

    def rcopy(src, dst, ss, rs, dev):
        return pltpu.make_async_remote_copy(
            src_ref=src, dst_ref=dst, send_sem=ss, recv_sem=rs, device_id=dev, device_id_type=MESH
        )

    def send(ref, ss, rs, dev):
        rcopy(ref, ref, ss, rs, dev).start()

    def arrived(ref, sem):
        pltpu.make_async_copy(ref, ref, sem).wait()

    def wrows(k, blk, half=None):
        if half is None:
            return W[k].at[pl.ds(pl.multiple_of(blk * 256, 256), 256)]
        return W[k].at[pl.ds(pl.multiple_of(blk * 256 + half * 128, 128), 128)]

    def chan(core, k):
        return pl.ds(pl.multiple_of(core * HALF + STARTS[k], CH), WIDTHS[k])

    def lanes(core, sub):
        return pl.ds(pl.multiple_of(core * HALF + sub * CH, CH), CH)

    def trows(core, half=None):
        if half is None:
            return pl.ds(pl.multiple_of(core * TOK, TOK), TOK)
        return pl.ds(pl.multiple_of(core * TOK + half * 256, 256), 256)

    def tcols(xx):
        return pl.ds(pl.multiple_of(lax.rem(xx, RING) * FEAT, FEAT), FEAT)

    barrier = pltpu.get_barrier_semaphore()

    for d in (right, left, up, down, xr, xl, sib):
        pl.semaphore_signal(barrier, inc=1, device_id=d, device_id_type=MESH)
    mine = pl.ds(pl.multiple_of(q * 256 + c * 128, 128), 128)
    own_tok = pltpu.make_async_copy(tok_hbm, X.at[trows(c), tcols(x)], local_sem.at[CHUNKS])
    for k in range(CHUNKS):
        for g in range(3):
            pltpu.make_async_copy(
                w_hbm.at[g, :, chan(c, k)],
                W[k].at[mine, pl.ds(g * WIDTHS[k], WIDTHS[k])],
                local_sem.at[k],
            ).start()
    own_tok.start()
    small = [
        pltpu.make_async_copy(src, dst, local_sem.at[CHUNKS + 1 + n])
        for n, (src, dst) in enumerate(((bias_hbm, bias), (rec_hbm, rec), (init_hbm, init)))
    ]
    for cp in small:
        cp.start()

    pl.semaphore_wait(barrier, 7)

    def own_rows(k):
        arrived(wrows(k, q, c), local_sem.at[k])
        send(wrows(k, q, c), w_s.at[k], p1_r.at[k, 0], right)
        send(wrows(k, q, c), w_s.at[k], p1_r.at[k, 1], left)

    for k in range(CHUNKS):
        for g in range(3):
            rcopy(
                w_hbm.at[g, :, chan(1 - c, k)],
                W[k].at[mine, pl.ds(g * WIDTHS[k], WIDTHS[k])],
                sib_s.at[k], sib_r.at[k], sib,
            ).start()
        if k == 0:
            own_rows(0)
    own_tok.wait()
    for h in range(2):
        send(X.at[trows(c, h), tcols(x)], t_s.at[0, h], t_r.at[0, h], xr)
        send(X.at[trows(c, 1 - h), tcols(x)], t_s.at[1, 1 - h], t_r.at[1, 1 - h], xl)
    send(X.at[trows(c), tcols(x)], ts_s.at[0], ts_r.at[0], sib)

    def send2(k, i):
        own = block(p + i, s)
        send(wrows(k, own, 0), w_s.at[k], p2_r.at[k, i, 0], up)
        send(wrows(k, own, 1), w_s.at[k], p2_r.at[k, i, 1], down)

    def send2b(k, i):
        own = block(p + i, s)
        send(wrows(k, own, 1), w_s.at[k], p2_r.at[k, i, 4], up)
        send(wrows(k, own, 0), w_s.at[k], p2_r.at[k, i, 5], down)

    def sibling_rows(k):
        arrived(wrows(k, q, 1 - c), sib_r.at[k])
        send(wrows(k, q, 1 - c), w_s.at[k], p1_r.at[k, 2], right)
        send(wrows(k, q, 1 - c), w_s.at[k], p1_r.at[k, 3], left)

    def ring_on(k):
        arrived(wrows(k, block(p + 3, s), c), p1_r.at[k, 0])
        send(wrows(k, block(p + 3, s), c), w_s.at[k], p1_r.at[k, 4], right)
        arrived(wrows(k, block(p + 1, s), c), p1_r.at[k, 1])
        arrived(wrows(k, block(p + 1, s), 1 - c), p1_r.at[k, 3])
        send(wrows(k, block(p + 1, s), 1 - c), w_s.at[k], p1_r.at[k, 5], left)
        arrived(wrows(k, block(p + 3, s), 1 - c), p1_r.at[k, 2])

    def ring_end(k):
        arrived(wrows(k, block(p + 2, s), c), p1_r.at[k, 4])
        arrived(wrows(k, block(p + 2, s), 1 - c), p1_r.at[k, 5])

    def pass_on(k, i):
        below, above = block(p + i, s + 3), block(p + i, s + 1)
        arrived(wrows(k, below, 0), p2_r.at[k, i, 0])
        send(wrows(k, below, 0), w_s.at[k], p2_r.at[k, i, 2], up)
        arrived(wrows(k, above, 1), p2_r.at[k, i, 1])
        send(wrows(k, above, 1), w_s.at[k], p2_r.at[k, i, 3], down)

    def near(k, i):
        arrived(wrows(k, block(p + i, s + 3), 1), p2_r.at[k, i, 4])
        arrived(wrows(k, block(p + i, s + 1), 0), p2_r.at[k, i, 5])

    def far(k, i):
        for h in range(2):
            arrived(wrows(k, block(p + i, s + 2), h), p2_r.at[k, i, 2 + h])

    def gathered(k):
        for i in ORDER:
            near(k, i)
            far(k, i)

    def features_first():
        arrived(X.at[trows(c, 0), tcols(x + 3)], t_r.at[0, 0])
        send(X.at[trows(c, 0), tcols(x + 3)], t_s.at[2, 0], t_r.at[2, 0], xr)
        arrived(X.at[trows(c, 1), tcols(x + 1)], t_r.at[1, 1])
        send(X.at[trows(c, 1), tcols(x + 1)], t_s.at[2, 1], t_r.at[2, 1], xl)
        send(X.at[trows(c, 0), tcols(x + 3)], ts_s.at[1], ts_r.at[1], sib)
        send(X.at[trows(c, 1), tcols(x + 1)], ts_s.at[2], ts_r.at[2], sib)

    def features_second():
        arrived(X.at[trows(c, 1), tcols(x + 3)], t_r.at[0, 1])
        send(X.at[trows(c, 1), tcols(x + 3)], ts_s.at[3], ts_r.at[3], sib)
        arrived(X.at[trows(c, 0), tcols(x + 1)], t_r.at[1, 0])
        send(X.at[trows(c, 0), tcols(x + 1)], ts_s.at[4], ts_r.at[4], sib)

    def features_last():
        for h in range(2):
            arrived(X.at[trows(c, h), tcols(x + 2)], t_r.at[2, h])
            send(X.at[trows(c, h), tcols(x + 2)], ts_s.at[5 + h], ts_r.at[5 + h], sib)

    def sibling_features():
        arrived(X.at[trows(1 - c), tcols(x)], ts_r.at[0])
        for n, (h, d) in enumerate(((0, 3), (1, 1), (1, 3), (0, 1))):
            arrived(X.at[trows(1 - c, h), tcols(x + d)], ts_r.at[1 + n])

    def sibling_last():
        for h in range(2):
            arrived(X.at[trows(1 - c, h), tcols(x + 2)], ts_r.at[5 + h])

    def row_of(ref, g, sub):
        return ref[pl.ds(g, 1), lanes(c, sub)]

    def put(k, acc, t, add):
        m = c if t < 2 else 1 - c
        for n, sub in enumerate(SUBS[k]):
            for g in range(3):
                v = acc[:, g * WIDTHS[k] + n * CH : g * WIDTHS[k] + (n + 1) * CH]
                if not add:
                    v = v + row_of(bias, g, sub)
                for h in range(SEGS // 2):
                    at = pl.ds((t % 2) * (SEGS // 2) + h, SEG, stride=SEGS)
                    part = v[h * SEG : (h + 1) * SEG]
                    PRE[sub, g, m, at, :] = PRE[sub, g, m, at, :] + part if add else part

    def quarter(t):
        return trows(c if t < 2 else 1 - c, t % 2)

    def matmul(k, t, places, add):
        cols = [tcols(x + d) for d in places]
        a = jnp.concatenate([X[quarter(t), d] for d in cols], axis=1)
        b = jnp.concatenate([W[k][d, :] for d in cols], axis=0)
        put(k, jnp.dot(a, b, preferred_element_type=jnp.float32), t, add)

    def matmul_part(k, t, chips, add):
        at = [pl.ds(pl.multiple_of(block(p + i, s + o) * 256, 256), 256) for i, o in chips]
        a = jnp.concatenate([X[quarter(t), d] for d in at], axis=1)
        b = jnp.concatenate([W[k][d, :] for d in at], axis=0)
        put(k, jnp.dot(a, b, preferred_element_type=jnp.float32), t, add)

    def vreg(j):
        return pl.ds(pl.multiple_of(j * SEGS, SEGS), SEGS)

    sublane = lax.broadcasted_iota(jnp.int32, (SEGS, CH), 0)

    def coefs(sub):
        return [jnp.broadcast_to(row_of(rec, g, sub), (SEGS, CH)) for g in range(3)]

    def publish(n, sub, AB):
        tot = []
        for m in range(2):
            SEGT[n, sub, m, 0], SEGT[n, sub, m, 1] = AB[m]
            ta, tb = SEGT[n, sub, m, 0, 0:1], SEGT[n, sub, m, 1, 0:1]
            for i in range(1, SEGS):
                a, b = SEGT[n, sub, m, 0, i : i + 1], SEGT[n, sub, m, 1, i : i + 1]
                ta, tb = a * ta, a * tb + b
            tot.append((ta, tb))
        (a0, b0), (a1, b1) = tot
        MID[n, sub] = jnp.where(sublane == 0, a0, b0)
        SUM[n, sub] = jnp.where(sublane == 0, a0 * a1, a1 * b0 + b1)

    def span(k):
        return pl.ds(*PASSES[k])

    def exchange(n, k):
        for dy, dz in FAR_FIRST:
            there = lax.rem(y + dy, RING) * RING + lax.rem(z + dz, RING)
            rcopy(
                SUM.at[n, span(k)], SLOT.at[n, lax.rem(there - q + CHIPS, CHIPS), span(k)],
                ex_s.at[n, k], ex_r.at[n, k], peer(there),
            ).start()

    def exchanged(n, k, sem):
        arrived(SLOT.at[n, pl.ds(1, CHIPS - 1), span(k)], sem.at[n, k])

    def incoming(n, sub):
        h = row_of(init, 0, sub)
        for e in range(CHIPS - 1, 0, -1):
            h = jnp.where(e <= q, SLOT[n, e, sub, 0:1] * h + SLOT[n, e, sub, 1:2], h)
        starts = [h, MID[n, sub, 0:1] * h + MID[n, sub, 1:2]]
        for m in range(2):
            h = starts[m]
            SEGT[n, sub, m, 2, 0:1] = h
            for i in range(SEGS - 1):
                h = SEGT[n, sub, m, 0, i : i + 1] * h + SEGT[n, sub, m, 1, i : i + 1]
                SEGT[n, sub, m, 2, i + 1 : i + 2] = h
        return [SEGT[n, sub, m, 2] for m in range(2)]

    UN = 16

    def pass1(sub):
        coef = coefs(sub)
        first = (sublane + q) == 0
        p0 = jnp.where(first, jnp.broadcast_to(row_of(init, 0, sub), (SEGS, CH)), 0.0)

        def step(j, AB, p0=None):
            new = []
            for m in range(2):
                v = vreg(j)
                pre = [PRE[sub, g, m, v, :] for g in range(3)]
                a, b = cell_at_zero(pre, coef) if p0 is None or m else cell(pre, p0, coef)
                AB1[sub, 0, m, v, :] = a
                AB1[sub, 1, m, v, :] = b
                new.append((a, b) if AB is None else (a * AB[m][0], a * AB[m][1] + b))
            return new

        AB = step(0, None, p0)
        for j in range(1, UN):
            AB = step(j, AB)

        def group(t, AB):
            for o in range(UN):
                AB = step(t * UN + o, AB)
            return AB

        publish(0, sub, lax.fori_loop(1, SEG // UN, group, AB))

    def pass2(sub):
        coef = coefs(sub)

        def group(t, carry):
            for o in range(UN):
                v = vreg(t * UN + o)
                new = []
                for m in range(2):
                    h, A, B = carry[m]
                    a, b = cell([PRE[sub, g, m, v, :] for g in range(3)], h, coef)
                    AB2[sub, 0, m, v, :] = a
                    AB2[sub, 1, m, v, :] = b
                    h = AB1[sub, 0, m, v, :] * h + AB1[sub, 1, m, v, :]
                    new.append((h, a * A, a * B + b))
                carry = new
            return carry

        one, zero = jnp.ones((SEGS, CH), jnp.float32), jnp.zeros((SEGS, CH), jnp.float32)
        carry = lax.fori_loop(0, SEG // UN, group, [(h, one, zero) for h in incoming(0, sub)])
        publish(1, sub, [(A, B) for _, A, B in carry])

    def pass3(sub):
        incoming(1, sub)
        here = out.at[:, lanes(c, sub)]

        def tokens_of(m):
            def group(t, h):
                for o in range(UN):
                    j = t * UN + o
                    v = vreg(j)
                    h = AB2[sub, 0, m, v, :] * h + AB2[sub, 1, m, v, :]
                    OUTB[sub, pl.ds(m * TOK + j, SEGS, stride=SEG), :] = h
                return h

            lax.fori_loop(0, SEG // UN, group, SEGT[1, sub, m, 2])

        tokens_of(1 - c)
        rcopy(OUTB.at[sub, trows(1 - c)], here, o_s.at[sub], o_r.at[sub], sib).start()
        tokens_of(c)
        pltpu.make_async_copy(OUTB.at[sub, trows(c)], here, o_l.at[sub]).start()

    def put_out(sub):
        here, there = out.at[:, lanes(c, sub)], out.at[:, lanes(1 - c, sub)]
        arrived(here, o_l.at[sub])
        arrived(here, o_s.at[sub])
        arrived(there, o_r.at[sub])

    def first_pass(k):
        for sub in SUBS[k]:
            pass1(sub)
        if k > 0:
            exchange(0, k - 1)

    def second_pass(k):
        exchanged(0, k, ex_r)
        for sub in range(PASSES[k][0], sum(PASSES[k])):
            pass2(sub)
        exchange(1, k)

    def last_pass(k):
        exchanged(1, k, ex_r)
        for sub in range(PASSES[k][0], sum(PASSES[k])):
            pass3(sub)

    def sent(k):
        arrived(wrows(k, q, c), sib_s.at[k])
        arrived(W[k].at[pl.ds(0, 30 * 128)], w_s.at[k])

    def sent_features():
        for h in range(2):
            for d in range(3):
                arrived(X.at[trows(c, h), tcols(x)], t_s.at[d, h])
        arrived(X.at[trows(c), tcols(x)], ts_s.at[0])
        for n in range(6):
            arrived(X.at[trows(c, 0), tcols(x)], ts_s.at[1 + n])

    sibling_rows(0)
    send2(0, 0)
    send2b(0, 0)
    ring_on(0)
    for i in (3, 1):
        send2(0, i)
        send2b(0, i)
    ring_end(0)
    send2(0, 2)
    send2b(0, 2)
    features_first()
    for cp in small:
        cp.wait()
    pass_on(0, 0)
    pass_on(0, 3)
    own_rows(1)
    sibling_rows(1)
    pass_on(0, 1)
    pass_on(0, 2)
    features_second()
    ring_on(1)
    ring_end(1)
    for i in ORDER:
        send2(1, i)
        send2b(1, i)
    own_rows(2)
    sibling_rows(2)
    gathered(0)
    matmul(0, 0, (0, 3, 1), False)
    ring_on(2)
    matmul(0, 1, (0, 3, 1), False)
    ring_end(2)
    send2(2, 0)
    send2b(2, 0)
    pass_on(1, 0)
    sibling_features()
    matmul(0, 2, (0, 3, 1), False)
    features_last()
    pass_on(1, 3)
    matmul(0, 3, (0, 3, 1), False)
    pass_on(1, 1)
    send2(2, 3)
    send2b(2, 3)
    matmul(0, 0, (2,), True)
    matmul(0, 1, (2,), True)
    pass_on(1, 2)
    sibling_last()
    matmul(0, 2, (2,), True)
    matmul(0, 3, (2,), True)
    first_pass(0)
    for i in (1, 2):
        send2(2, i)
        send2b(2, i)
    for i in ORDER:
        near(1, i)
    for t in range(4):
        matmul_part(1, t, [(i, o) for o in (0, 1, 3) for i in ORDER], False)
        if t % 2 == 1:
            pass_on(2, ORDER[t // 2])
    for i in ORDER:
        far(1, i)
    for t in range(4):
        matmul_part(1, t, [(i, 2) for i in ORDER], True)
    first_pass(1)
    pass_on(2, 1)
    pass_on(2, 2)
    for i in ORDER:
        near(2, i)
    for t in range(4):
        matmul_part(2, t, [(i, o) for o in (0, 1, 3) for i in ORDER], False)
    far(2, 0)
    far(2, 3)
    for t in range(4):
        matmul_part(2, t, [(i, 2) for i in (0, 3)], True)
    far(2, 1)
    far(2, 2)
    for t in range(4):
        matmul_part(2, t, [(i, 2) for i in (1, 2)], True)
    first_pass(2)
    second_pass(0)
    second_pass(1)
    for k in range(CHUNKS):
        sent(k)
    sent_features()
    exchanged(0, 0, ex_s)
    exchanged(0, 1, ex_s)
    last_pass(0)
    exchanged(1, 0, ex_s)
    last_pass(1)
    exchanged(1, 1, ex_s)
    for sub in range(GROUPS):
        put_out(sub)


def copy_out(src, dst, store):
    rows = TOK // 8
    outs = [
        pltpu.make_async_copy(src.at[pl.ds(i * rows, rows)], dst.at[pl.ds(i * rows, rows)], store.at[i])
        for i in range(8)
    ]
    for cp in outs:
        cp.start()
    for cp in outs:
        cp.wait()


def body(tokens, weights, gate_bias, recurrent, initial_state):
    dma = pltpu.SemaphoreType.DMA
    f32, bf16 = jnp.float32, jnp.bfloat16
    hbm = pl.BlockSpec(memory_space=pl.ANY)
    args = (tokens, weights, gate_bias, recurrent, initial_state[None, :])
    args = [pltpu.with_memory_space_constraint(a, pltpu.HBM) for a in args]
    states = pl.pallas_call(
        kernel,
        out_shape=jax.ShapeDtypeStruct((TOK, 2 * HALF), f32),
        in_specs=[hbm] * 5,
        out_specs=hbm,
        scratch_shapes=[
            pltpu.VMEM((ROWS, DEPTH), bf16),
            *[pltpu.VMEM((DEPTH, 3 * w), bf16) for w in WIDTHS],
            pltpu.VMEM((3, 2 * HALF), f32),
            pltpu.VMEM((3, 2 * HALF), f32),
            pltpu.VMEM((1, 2 * HALF), f32),
            pltpu.VMEM((GROUPS, 3, 2, TOK, CH), f32),
            pltpu.VMEM((GROUPS, 2, 2, TOK, CH), f32),
            pltpu.VMEM((GROUPS, 2, 2, TOK, CH), f32),
            pltpu.VMEM((GROUPS, ROWS, CH), f32),
            pltpu.VMEM((2, GROUPS, 2, 3, SEGS, CH), f32),
            pltpu.VMEM((2, GROUPS, SEGS, CH), f32),
            pltpu.VMEM((2, GROUPS, SEGS, CH), f32),
            pltpu.VMEM((2, CHIPS, GROUPS, SEGS, CH), f32),
            dma((CHUNKS + 4,)),
            dma((CHUNKS,)),
            dma((CHUNKS,)),
            dma((CHUNKS,)),
            dma((CHUNKS, 6)),
            dma((CHUNKS, RING, 6)),
            dma((3, 2)),
            dma((3, 2)),
            dma((7,)),
            dma((7,)),
            dma((2, len(PASSES))),
            dma((2, len(PASSES))),
            dma((GROUPS,)),
            dma((GROUPS,)),
            dma((GROUPS,)),
        ],
        compiler_params=pltpu.CompilerParams(
            collective_id=0, has_side_effects=True, vmem_limit_bytes=47 * 2**20
        ),
        cost_estimate=pl.CostEstimate(
            flops=2 * ROWS * DEPTH * 3 * HALF, bytes_accessed=8 * 2**20, transcendentals=0
        ),
    )(*args)
    return pl.pallas_call(
        copy_out,
        out_shape=jax.ShapeDtypeStruct((TOK, 2 * HALF), f32),
        in_specs=[pl.BlockSpec(memory_space=pltpu.VMEM)],
        out_specs=hbm,
        scratch_shapes=[dma((8,))],
        compiler_params=pltpu.CompilerParams(vmem_limit_bytes=16 * 2**20),
    )(states)


def solution(mesh):
    return jax.shard_map(
        body,
        mesh=mesh,
        in_specs=(P("seq", "tp"), P(None, "seq", "tp"), P(None, "tp"), P(None, "tp"), P("tp")),
        out_specs=P("seq", "tp"),
        check_vma=False,
    )
```
